32 devices in a mesh: replica: 8 (over z, core), shard: 4 (over y, x).
Axes of the slice: x: 2, y: 2, z: 4, core: 2. Of those that a mesh axis runs over, the one named last changes fastest.
Arguments:
- context_one: bfloat16 [2048, 5120], P('replica', 'shard'), may hold values from -8 to 8
- cotangent_one: bfloat16 [2048, 5120], P('replica', 'shard'), may hold values from -32 to 32
- context_two: bfloat16 [2048, 5120], P('replica', 'shard'), may hold values from -8 to 8
- cotangent_two: bfloat16 [2048, 5120], P('replica', 'shard'), may hold values from -32 to 32
Outputs:
- combined_one: float32 [5120, 5120], P('shard', 'replica')
- combined_two: float32 [5120, 5120], P('shard', 'replica')
The draws below stay inside these ranges and needn't reach their ends.
All inputs are finite; a program needn't handle non-finite values.
Results may differ from the reference program's by a relative error of at most 0.0047.
Values may be sent and summed in bfloat16 or wider, within the bound.
A program may use at most 128 MiB of HBM per device.

```python
import jax
import jax.numpy as jnp

D = 5120
TOK_REP = 256
N_REPLICA = 8


def mixed_rows(key, scale, spread):
    base_key, noise_key, share_key, column_key, feature_key = jax.random.split(key, 5)
    base = jax.random.normal(base_key, (TOK_REP, D), jnp.float32)
    noise = jax.random.normal(noise_key, (N_REPLICA, TOK_REP, D), jnp.float32)
    ramp = jnp.arange(N_REPLICA, dtype=jnp.float32) / float(max(N_REPLICA - 1, 1))
    jitter = jax.random.uniform(share_key, (N_REPLICA,), jnp.float32, 0.85, 1.0)
    feature_ramp = jnp.arange(D, dtype=jnp.float32) / float(max(D - 1, 1))
    feature_jitter = jax.random.uniform(feature_key, (D,), jnp.float32, 0.8, 1.0)
    feature_share = (0.1 + 0.9 * feature_ramp) * feature_jitter
    share = ((0.15 + 0.7 * ramp) * jitter)[:, None, None] * feature_share[None, None, :]
    columns = jnp.exp(jax.random.uniform(column_key, (D,), jnp.float32, -spread, spread))
    values = (jnp.sqrt(share) * base[None] + jnp.sqrt(1.0 - share) * noise) * columns * scale
    values = jnp.clip(values, -8.0 * scale, 8.0 * scale)
    return values.reshape(N_REPLICA * TOK_REP, D)


def draw_context_one(key, part):
    key = jax.random.fold_in(key, 11)
    return mixed_rows(key, 1.0, 0.35).astype(jnp.bfloat16)


def draw_cotangent_one(key, part):
    key = jax.random.fold_in(key, 12)
    return mixed_rows(key, 4.0, 0.35).astype(jnp.bfloat16)


def draw_context_two(key, part):
    key = jax.random.fold_in(key, 13)
    return mixed_rows(key, 1.0, 0.35).astype(jnp.bfloat16)


def draw_cotangent_two(key, part):
    key = jax.random.fold_in(key, 14)
    return mixed_rows(key, 4.0, 0.35).astype(jnp.bfloat16)


def setup_inputs(seed: int = 0) -> dict:
    seeds = jax.random.split(jax.random.key(seed), 5)
    context_one = draw_context_one(jax.random.fold_in(seeds[4], 71), 0)
    cotangent_one = draw_cotangent_one(jax.random.fold_in(seeds[4], 71), 0)
    context_two = draw_context_two(jax.random.fold_in(seeds[4], 71), 0)
    cotangent_two = draw_cotangent_two(jax.random.fold_in(seeds[4], 71), 0)
    return dict(context_one=context_one, cotangent_one=cotangent_one, context_two=context_two, cotangent_two=cotangent_two)


EPSILON = 1e-6


def adasum_pair(lower_part, upper_part, final):
    lower_f = lower_part.astype(jnp.float32)
    upper_f = upper_part.astype(jnp.float32)
    inner_sum = jnp.sum(lower_f * upper_f)
    lower_sq = jnp.sum(lower_f * lower_f)
    upper_sq = jnp.sum(upper_f * upper_f)
    coeff_lower = 1.0 - inner_sum / (2.0 * (lower_sq + EPSILON))
    coeff_upper = 1.0 - inner_sum / (2.0 * (upper_sq + EPSILON))
    combined = coeff_lower * lower_f + coeff_upper * upper_f
    if final:
        return combined
    return combined.astype(jnp.bfloat16)


def replica_gradient(context, cotangent, first_index):
    rows_context = context[first_index * TOK_REP:(first_index + 1) * TOK_REP]
    rows_cotangent = cotangent[first_index * TOK_REP:(first_index + 1) * TOK_REP]
    product = jnp.dot(rows_context.T, rows_cotangent, preferred_element_type=jnp.float32)
    return (product / float(TOK_REP)).astype(jnp.bfloat16)


def combine_range(context, cotangent, first_index, span_count, final):
    if span_count == 1:
        return replica_gradient(context, cotangent, first_index)
    half_count = span_count // 2
    lower_part = combine_range(context, cotangent, first_index, half_count, False)
    upper_part = combine_range(context, cotangent, first_index + half_count, half_count, False)
    return adasum_pair(lower_part, upper_part, final)


def reference(context_one, cotangent_one, context_two, cotangent_two):
    combined_one = combine_range(context_one, cotangent_one, 0, N_REPLICA, True)
    combined_two = combine_range(context_two, cotangent_two, 0, N_REPLICA, True)
    return (combined_one, combined_two)
```

```python
import functools

import jax
import jax.numpy as jnp
from jax import lax
from jax.experimental import pallas as pl
from jax.experimental.pallas import tpu as pltpu
from jax.sharding import PartitionSpec as P

EPSILON = 1e-06
MESH = pl.DeviceIdType.MESH
LAYERS = 2
LANES = 128
F32 = jnp.float32


def pair_coefficient(inner, own_sq, other_sq):
    own_sq = jnp.maximum(own_sq, 0.0)
    bound = jnp.sqrt(own_sq) * jnp.sqrt(jnp.maximum(other_sq, 0.0))
    inner = jnp.clip(inner, -bound, bound)
    return 1.0 - inner / (2.0 * (own_sq + EPSILON))


def replica_weights(gram, n):
    row = lax.broadcasted_iota(jnp.int32, gram.shape, 0)
    lane = lax.broadcasted_iota(jnp.int32, gram.shape, 1)
    col_w = jnp.ones((n, 1), F32)
    row_w = jnp.ones((1, LANES), F32)
    for level in range(n.bit_length() - 1):
        same = (row >> level) == (lane >> level)
        other = (row >> level) == ((lane >> level) ^ 1)
        scaled = gram * col_w * row_w
        inside = jnp.where(same, scaled, 0.0)
        across = jnp.where(other, scaled, 0.0)
        in_row = jnp.sum(inside, axis=0, keepdims=True)
        ac_row = jnp.sum(across, axis=0, keepdims=True)
        in_col = jnp.sum(inside, axis=1, keepdims=True)
        ac_col = jnp.sum(across, axis=1, keepdims=True)

        def total(mask, value, axis):
            return jnp.sum(jnp.where(mask, value, 0.0), axis=axis, keepdims=True)

        col_w = col_w * pair_coefficient(
            total(same, ac_row, 1), total(same, in_row, 1), total(other, in_row, 1)
        )
        row_w = row_w * pair_coefficient(
            total(same, ac_col, 0), total(same, in_col, 0), total(other, in_col, 0)
        )
    return col_w


def kernel(
    n, ns, tok, cols, ocols, mt,
    c1, t1, c2, t2, out1, out2,
    c_all, t_all, stage, t_scaled, obuf, acc, ar1, ar2, mine,
    loc_sem, tl_sem, ta_send, ta_recv, tb_loc, tb_send, tb_recv, tc_send, tc_recv,
    c_send, c_recv, sib_send, sib_recv, a1_send, a1_recv, a2_send, a2_recv, osem,
):
    nz = n // 2
    tq = tok // ns
    c_in, t_in, outs = (c1, c2), (t1, t2), (out1, out2)
    r = lax.axis_index("replica")
    s = lax.axis_index("shard")
    z = r // 2
    core = r % 2
    sib = z * 2 + 1 - core
    layers = range(LAYERS)

    def remote(src, dst, ss, rs, dr, ds):
        return pltpu.make_async_remote_copy(
            src_ref=src, dst_ref=dst, send_sem=ss, recv_sem=rs,
            device_id=(dr, ds), device_id_type=MESH,
        )

    def rows(rep):
        return pl.ds(pl.multiple_of(rep * tok, tok), tok)

    def quarter(q):
        return pl.ds(pl.multiple_of(q * tq, tq), tq)

    def t_half(l, q, h):
        if ocols % LANES == 0:
            return t_in[l].at[quarter(q), pl.ds(h * ocols, ocols)]
        return t_in[l].at[h, quarter(q)]

    barrier = pltpu.get_barrier_semaphore()
    for q in range(ns):
        @pl.when(q != s)
        def _():
            pl.semaphore_signal(barrier, inc=1, device_id=(r, q), device_id_type=MESH)
    for rep in range(n):
        @pl.when(rep != r)
        def _():
            pl.semaphore_signal(barrier, inc=1, device_id=(rep, s), device_id_type=MESH)
    local = []
    for l in layers:
        local.append(pltpu.make_async_copy(c_in[l], c_all.at[l, rows(r)], loc_sem.at[l]))
        for h in range(2):
            local.append(pltpu.make_async_copy(t_half(l, s, h), stage.at[l, s, h], tl_sem.at[l, h]))
    for copy in local:
        copy.start()
    pl.semaphore_wait(barrier, n + ns - 2)

    def ta(l, q, h):
        return remote(t_half(l, q, h), stage.at[l, s, h], ta_send.at[l, q, h],
                      ta_recv.at[l, s, h], r, q)

    def ta_in(l, q, h):
        return remote(t_half(l, s, h), stage.at[l, q, h], ta_send.at[l, q, h],
                      ta_recv.at[l, q, h], r, q)

    def tb(l, j):
        return remote(stage.at[l, j // 2, j % 2], t_all.at[l, r, quarter(s)],
                      tb_send.at[l, j], tb_recv.at[l, r], j, s)

    def tb_in(l, j):
        return remote(stage.at[l, j // 2, j % 2], t_all.at[l, j, quarter(s)],
                      tb_send.at[l, j], tb_recv.at[l, j], j, s)

    def tb_own(l, j):
        return pltpu.make_async_copy(stage.at[l, j // 2, j % 2], t_all.at[l, r, quarter(s)], tb_loc.at[l])

    def tc(l, q):
        part = t_all.at[l, :, quarter(s)]
        return remote(part, part, tc_send.at[l, q], tc_recv.at[l, s], r, q)

    def tc_in(l, q):
        part = t_all.at[l, :, quarter(q)]
        return remote(part, part, tc_send.at[l, q], tc_recv.at[l, q], r, q)

    def c_copy(l, way, t):
        chip = z - t if way == 0 else z + t
        block = c_all.at[l, rows(2 * chip + core)]
        src = c_in[l] if t == 0 else block
        to = r + 2 if way == 0 else r - 2
        return remote(src, block, c_send.at[l, way, t], c_recv.at[l, way, t], to, s)

    def c_sends(way, t):
        if way == 0:
            return jnp.logical_and(z < nz - 1, z - t >= 0)
        return jnp.logical_and(z > 0, z + t <= nz - 1)

    def c_in_chip(way, t):
        return z - 1 - t if way == 0 else z + 1 + t

    def c_valid(way, t):
        chip = c_in_chip(way, t)
        return chip >= 0 if way == 0 else chip <= nz - 1

    def c_wait(l, way, t):
        block = c_all.at[l, rows(2 * c_in_chip(way, t) + core)]
        remote(block, block, c_send.at[l, way, t], c_recv.at[l, way, t], sib, s).wait_recv()

    def sib_out(l, chip):
        block = c_all.at[l, rows(2 * chip + core)]
        return remote(block, block, sib_send.at[l, chip], sib_recv.at[l, chip], sib, s)

    def sib_in(l, chip):
        block = c_all.at[l, rows(2 * chip + 1 - core)]
        return remote(block, block, sib_send.at[l, chip], sib_recv.at[l, chip], sib, s)

    def when_each(pairs):
        for cond, fn in pairs:
            pl.when(cond)(fn)

    for l in layers:
        for q in range(ns):
            for h in range(2):
                when_each([(q != s, lambda l=l, q=q, h=h: ta(l, q, h).start())])
        for way in range(2):
            when_each([(c_sends(way, 0), lambda l=l, way=way: c_copy(l, way, 0).start())])
    for copy in local:
        copy.wait()
    for l in layers:
        sib_out(l, z).start()

    for l in layers:
        for q in range(ns):
            for h in range(2):
                when_each([(q != s, lambda l=l, q=q, h=h: ta_in(l, q, h).wait_recv())])
        for j in range(n):
            when_each([
                (j != r, lambda l=l, j=j: tb(l, j).start()),
                (j == r, lambda l=l, j=j: tb_own(l, j).start()),
            ])

    def arrive(l, t):
        for way in range(2):
            def take(l=l, way=way, t=t):
                c_wait(l, way, t)
                if t + 1 <= nz - 2:
                    when_each([(c_sends(way, t + 1), lambda: c_copy(l, way, t + 1).start())])
                sib_out(l, c_in_chip(way, t)).start()

            when_each([(c_valid(way, t), take)])

    def share_t(l):
        for j in range(n):
            when_each([
                (j != r, lambda l=l, j=j: tb_in(l, j).wait_recv()),
                (j == r, lambda l=l, j=j: tb_own(l, j).wait()),
            ])
        for q in range(ns):
            when_each([(q != s, lambda l=l, q=q: tc(l, q).start())])

    for t in range(max(nz - 2, 1)):
        for l in layers:
            arrive(l, t)
            if t == 0:
                share_t(l)

    def gram_block(l, i, j):
        a = pl.ds(pl.multiple_of(i * 2 * tok, 2 * tok), 2 * tok)
        b = pl.ds(pl.multiple_of(j * 2 * tok, 2 * tok), 2 * tok)
        dims = (((1,), (1,)), ((), ()))
        x = lax.dot_general(c_all[l, a, :], c_all[l, b, :], dims, preferred_element_type=F32)
        ti = t_all[l, pl.ds(2 * i, 2)].reshape(2 * tok, ocols)
        tj = t_all[l, pl.ds(2 * j, 2)].reshape(2 * tok, ocols)
        y = lax.dot_general(ti, tj, dims, preferred_element_type=F32)
        p = x * y
        for da in range(2):
            part = jnp.sum(p[da * tok : (da + 1) * tok], axis=0, keepdims=True)
            for db in range(2):
                v = part[:, db * tok : db * tok + LANES]
                for e in range(1, tok // LANES):
                    v = v + part[:, db * tok + e * LANES : db * tok + (e + 1) * LANES]
                acc[l, 2 * i + da, pl.ds(2 * j + db, 1), :] = v
                acc[l, 2 * j + db, pl.ds(2 * i + da, 1), :] = v

    def gram_step(l, t):
        for way in range(2):
            when_each([(c_valid(way, t), lambda l=l, way=way, t=t: sib_in(l, c_in_chip(way, t)).wait_recv())])
        lo0, hi0 = jnp.maximum(z - t, 0), jnp.minimum(z + t, nz - 1)
        lo1, hi1 = jnp.maximum(z - 1 - t, 0), jnp.minimum(z + 1 + t, nz - 1)
        down = jnp.where(lo1 < lo0, hi0 - lo1 + 1, 0)
        up = jnp.where(hi1 > hi0, hi1 - lo1 + 1, 0)
        own = 1 if t == 0 else 0

        def body(k, _):
            i = jnp.where(k < own, z, jnp.where(k < own + down, lo1, lo1 + k - own - down))
            j = jnp.where(k < own, z, jnp.where(k < own + down, lo1 + k - own, hi1))
            gram_block(l, i, j)
            return 0

        lax.fori_loop(0, own + down + up, body, 0)

    def all_sum(l, value):
        ar1[l, s] = value
        mine[l, 0] = value
        for q in range(ns):
            when_each([(q != s, lambda q=q: remote(
                mine.at[l, 0], ar1.at[l, s], a1_send.at[l, q], a1_recv.at[l, s], r, q).start())])
        for q in range(ns):
            when_each([(q != s, lambda q=q: remote(
                mine.at[l, 0], ar1.at[l, q], a1_send.at[l, q], a1_recv.at[l, q], r, q).wait_recv())])
        value = jnp.sum(ar1[l], axis=0)
        ar2[l, r] = value
        mine[l, 1] = value
        for j in range(n):
            when_each([(j != r, lambda j=j: remote(
                mine.at[l, 1], ar2.at[l, r], a2_send.at[l, j], a2_recv.at[l, r], j, s).start())])
        for j in range(n):
            when_each([(j != r, lambda j=j: remote(
                mine.at[l, 1], ar2.at[l, j], a2_send.at[l, j], a2_recv.at[l, j], j, s).wait_recv())])
        return jnp.sum(ar2[l], axis=0)

    def out_copy(l, m):
        part = pl.ds(pl.multiple_of(m * mt, mt), mt)
        return pltpu.make_async_copy(obuf.at[l, part], outs[l].at[part], osem.at[l, m])

    def finish(l):
        lane = lax.broadcasted_iota(jnp.int32, (n, LANES), 1)
        gram = jnp.zeros((n, LANES), F32)
        for a in range(n):
            gram = jnp.where(lane == a, jnp.sum(acc[l, a], axis=1, keepdims=True), gram)
        gram = all_sum(l, gram) * (1.0 / (float(tok) * float(tok)))
        weights = replica_weights(gram, n) * (1.0 / float(tok))
        for rep in range(n):
            w = jnp.broadcast_to(weights[rep : rep + 1, :], (tok, ocols))
            t_scaled[rep * tok : (rep + 1) * tok, :] = (t_all[l, rep].astype(F32) * w).astype(jnp.bfloat16)

        def body(m, _):
            part = pl.ds(pl.multiple_of(m * mt, mt), mt)
            obuf[l, part, :] = lax.dot_general(
                c_all[l, :, part] if mt != cols else c_all[l],
                t_scaled[...], (((0,), (0,)), ((), ())), preferred_element_type=F32,
            )
            out_copy(l, m).start()
            return 0

        lax.fori_loop(0, cols // mt, body, 0)

    for l in layers:
        sib_in(l, z).wait_recv()
        for q in range(ns):
            when_each([(q != s, lambda l=l, q=q: tc_in(l, q).wait_recv())])
        for t in range(nz - 1):
            if t == nz - 2 and t > 0:
                arrive(l, t)
            gram_step(l, t)
        finish(l)

    for l in layers:
        for q in range(ns):
            def drain(l=l, q=q):
                for h in range(2):
                    ta(l, q, h).wait_send()
                tc(l, q).wait_send()
                remote(mine.at[l, 0], ar1.at[l, s], a1_send.at[l, q], a1_recv.at[l, s], r, q).wait_send()

            when_each([(q != s, drain)])
        for j in range(n):
            def drain_b(l=l, j=j):
                tb(l, j).wait_send()
                remote(mine.at[l, 1], ar2.at[l, r], a2_send.at[l, j], a2_recv.at[l, r], j, s).wait_send()

            when_each([(j != r, drain_b)])
        sib_out(l, z).wait_send()
        for t in range(nz - 1):
            for way in range(2):
                when_each([
                    (c_sends(way, t), lambda l=l, way=way, t=t: c_copy(l, way, t).wait_send()),
                    (c_valid(way, t), lambda l=l, way=way, t=t: sib_out(l, c_in_chip(way, t)).wait_send()),
                ])
        for m in range(cols // mt):
            out_copy(l, m).wait()


def solution(mesh):
    n, ns = mesh.shape["replica"], mesh.shape["shard"]

    def shards(context_one, cotangent_one, context_two, cotangent_two):
        tok, cols = context_one.shape
        ocols = cols * ns // n
        mt = 256 if cols % 256 == 0 else cols
        nz = n // 2

        def halves(t):
            if ocols % LANES == 0:
                return t
            return t.reshape(tok, 2, ocols).transpose(1, 0, 2)

        dma = lambda *shape: pltpu.SemaphoreType.DMA(shape)
        bf = jnp.bfloat16
        any_spec = pl.BlockSpec(memory_space=pl.ANY)
        flops = LAYERS * 2 * n * tok * (cols * ocols + n * tok * (cols + ocols) // 2)
        return pl.pallas_call(
            functools.partial(kernel, n, ns, tok, cols, ocols, mt),
            out_shape=[jax.ShapeDtypeStruct((cols, ocols), F32)] * 2,
            in_specs=[any_spec] * 4,
            out_specs=[any_spec] * 2,
            scratch_shapes=[
                pltpu.VMEM((LAYERS, n * tok, cols), bf),
                pltpu.VMEM((LAYERS, n, tok, ocols), bf),
                pltpu.VMEM((LAYERS, ns, 2, tok // ns, ocols), bf),
                pltpu.VMEM((n * tok, ocols), bf),
                pltpu.VMEM((LAYERS, cols, ocols), F32),
                pltpu.VMEM((LAYERS, n, n, LANES), F32),
                pltpu.VMEM((LAYERS, ns, n, LANES), F32),
                pltpu.VMEM((LAYERS, n, n, LANES), F32),
                pltpu.VMEM((LAYERS, 2, n, LANES), F32),
                dma(LAYERS), dma(LAYERS, 2),
                dma(LAYERS, ns, 2), dma(LAYERS, ns, 2),
                dma(LAYERS), dma(LAYERS, n), dma(LAYERS, n),
                dma(LAYERS, ns), dma(LAYERS, ns),
                dma(LAYERS, 2, nz), dma(LAYERS, 2, nz),
                dma(LAYERS, nz), dma(LAYERS, nz),
                dma(LAYERS, ns), dma(LAYERS, ns),
                dma(LAYERS, n), dma(LAYERS, n),
                dma(LAYERS, cols // mt),
            ],
            compiler_params=pltpu.CompilerParams(
                collective_id=0, has_side_effects=True, vmem_limit_bytes=56 * 2**20
            ),
            cost_estimate=pl.CostEstimate(
                flops=flops, transcendentals=0,
                bytes_accessed=LAYERS * (2 * tok * cols * 2 + cols * ocols * 4),
            ),
        )(context_one, halves(cotangent_one), context_two, halves(cotangent_two))

    return jax.shard_map(
        shards,
        mesh=mesh,
        in_specs=(P("replica", "shard"),) * 4,
        out_specs=(P("shard", "replica"),) * 2,
        check_vma=False,
    )
```

```python
import functools

import jax
import jax.numpy as jnp
from jax import lax
from jax.experimental import pallas as pl
from jax.experimental.pallas import tpu as pltpu
from jax.sharding import PartitionSpec as P

EPSILON = 1e-06
MESH = pl.DeviceIdType.MESH
LAYERS = 2
LANES = 128
F32 = jnp.float32


def pair_coefficient(inner, own_sq, other_sq):
    own_sq = jnp.maximum(own_sq, 0.0)
    bound = jnp.sqrt(own_sq) * jnp.sqrt(jnp.maximum(other_sq, 0.0))
    inner = jnp.clip(inner, -bound, bound)
    return 1.0 - inner / (2.0 * (own_sq + EPSILON))


def replica_weights(gram, n):
    row = lax.broadcasted_iota(jnp.int32, gram.shape, 0)
    lane = lax.broadcasted_iota(jnp.int32, gram.shape, 1)
    col_w = jnp.ones((n, 1), F32)
    row_w = jnp.ones((1, LANES), F32)
    for level in range(n.bit_length() - 1):
        same = (row >> level) == (lane >> level)
        other = (row >> level) == ((lane >> level) ^ 1)
        scaled = gram * col_w * row_w
        inside = jnp.where(same, scaled, 0.0)
        across = jnp.where(other, scaled, 0.0)
        in_row = jnp.sum(inside, axis=0, keepdims=True)
        ac_row = jnp.sum(across, axis=0, keepdims=True)
        in_col = jnp.sum(inside, axis=1, keepdims=True)
        ac_col = jnp.sum(across, axis=1, keepdims=True)

        def total(mask, value, axis):
            return jnp.sum(jnp.where(mask, value, 0.0), axis=axis, keepdims=True)

        col_w = col_w * pair_coefficient(
            total(same, ac_row, 1), total(same, in_row, 1), total(other, in_row, 1)
        )
        row_w = row_w * pair_coefficient(
            total(same, ac_col, 0), total(same, in_col, 0), total(other, in_col, 0)
        )
    return col_w


def kernel(
    n, ns, tok, cols, ocols, mt,
    c1, t1, c2, t2, out1, out2,
    c_all, t_all, stage, t_scaled, obuf, acc, ar1, ar2, mine,
    loc_sem, tl_sem, ta_send, ta_recv, tb_loc, tb_send, tb_recv, tc_send, tc_recv,
    c_send, c_recv, sib_send, sib_recv, a1_send, a1_recv, a2_send, a2_recv, osem,
):
    nz = n // 2
    tq = tok // ns
    c_in, t_in, outs = (c1, c2), (t1, t2), (out1, out2)
    r = lax.axis_index("replica")
    s = lax.axis_index("shard")
    z = r // 2
    core = r % 2
    sib = z * 2 + 1 - core
    layers = range(LAYERS)

    def remote(src, dst, ss, rs, dr, ds):
        return pltpu.make_async_remote_copy(
            src_ref=src, dst_ref=dst, send_sem=ss, recv_sem=rs,
            device_id=(dr, ds), device_id_type=MESH,
        )

    def rows(rep):
        return pl.ds(pl.multiple_of(rep * tok, tok), tok)

    def quarter(q):
        return pl.ds(pl.multiple_of(q * tq, tq), tq)

    def t_half(l, q, h):
        if ocols % LANES == 0:
            return t_in[l].at[quarter(q), pl.ds(h * ocols, ocols)]
        return t_in[l].at[h, quarter(q)]

    barrier = pltpu.get_barrier_semaphore()
    for q in range(ns):
        @pl.when(q != s)
        def _():
            pl.semaphore_signal(barrier, inc=1, device_id=(r, q), device_id_type=MESH)
    for rep in range(n):
        @pl.when(rep != r)
        def _():
            pl.semaphore_signal(barrier, inc=1, device_id=(rep, s), device_id_type=MESH)
    local = []
    for l in layers:
        local.append(pltpu.make_async_copy(c_in[l], c_all.at[l, rows(r)], loc_sem.at[l]))
        for h in range(2):
            local.append(pltpu.make_async_copy(t_half(l, s, h), stage.at[l, s, h], tl_sem.at[l, h]))
    for copy in local:
        copy.start()
    pl.semaphore_wait(barrier, n + ns - 2)

    def ta(l, q, h):
        return remote(t_half(l, q, h), stage.at[l, s, h], ta_send.at[l, q, h],
                      ta_recv.at[l, s, h], r, q)

    def ta_in(l, q, h):
        return remote(t_half(l, s, h), stage.at[l, q, h], ta_send.at[l, q, h],
                      ta_recv.at[l, q, h], r, q)

    def tb(l, j):
        return remote(stage.at[l, j // 2, j % 2], t_all.at[l, r, quarter(s)],
                      tb_send.at[l, j], tb_recv.at[l, r], j, s)

    def tb_in(l, j):
        return remote(stage.at[l, j // 2, j % 2], t_all.at[l, j, quarter(s)],
                      tb_send.at[l, j], tb_recv.at[l, j], j, s)

    def tb_own(l, j):
        return pltpu.make_async_copy(stage.at[l, j // 2, j % 2], t_all.at[l, r, quarter(s)], tb_loc.at[l])

    def tc(l, q):
        part = t_all.at[l, :, quarter(s)]
        return remote(part, part, tc_send.at[l, q], tc_recv.at[l, s], r, q)

    def tc_in(l, q):
        part = t_all.at[l, :, quarter(q)]
        return remote(part, part, tc_send.at[l, q], tc_recv.at[l, q], r, q)

    def c_copy(l, way, t):
        chip = z - t if way == 0 else z + t
        block = c_all.at[l, rows(2 * chip + core)]
        src = c_in[l] if t == 0 else block
        to = r + 2 if way == 0 else r - 2
        return remote(src, block, c_send.at[l, way, t], c_recv.at[l, way, t], to, s)

    def c_sends(way, t):
        if way == 0:
            return jnp.logical_and(z < nz - 1, z - t >= 0)
        return jnp.logical_and(z > 0, z + t <= nz - 1)

    def c_in_chip(way, t):
        return z - 1 - t if way == 0 else z + 1 + t

    def c_valid(way, t):
        chip = c_in_chip(way, t)
        return chip >= 0 if way == 0 else chip <= nz - 1

    def c_wait(l, way, t):
        block = c_all.at[l, rows(2 * c_in_chip(way, t) + core)]
        remote(block, block, c_send.at[l, way, t], c_recv.at[l, way, t], sib, s).wait_recv()

    def sib_out(l, chip):
        block = c_all.at[l, rows(2 * chip + core)]
        return remote(block, block, sib_send.at[l, chip], sib_recv.at[l, chip], sib, s)

    def sib_in(l, chip):
        block = c_all.at[l, rows(2 * chip + 1 - core)]
        return remote(block, block, sib_send.at[l, chip], sib_recv.at[l, chip], sib, s)

    def when_each(pairs):
        for cond, fn in pairs:
            pl.when(cond)(fn)

    def ta_start(l):
        for q in range(ns):
            for h in range(2):
                when_each([(q != s, lambda q=q, h=h: ta(l, q, h).start())])

    def own_start(l):
        for way in range(2):
            when_each([(c_sends(way, 0), lambda way=way: c_copy(l, way, 0).start())])

    def own_sent(l):
        for way in range(2):
            when_each([(c_sends(way, 0), lambda way=way: c_copy(l, way, 0).wait_send())])

    def tb_start(l):
        for q in range(ns):
            for h in range(2):
                when_each([(q != s, lambda q=q, h=h: ta_in(l, q, h).wait_recv())])
        for j in range(n):
            when_each([
                (j != r, lambda j=j: tb(l, j).start()),
                (j == r, lambda j=j: tb_own(l, j).start()),
            ])

    def arrive(l, t):
        for way in range(2):
            def take(l=l, way=way, t=t):
                c_wait(l, way, t)
                if t + 1 <= nz - 2:
                    when_each([(c_sends(way, t + 1), lambda: c_copy(l, way, t + 1).start())])
                sib_out(l, c_in_chip(way, t)).start()

            when_each([(c_valid(way, t), take)])

    def share_t(l):
        for j in range(n):
            when_each([
                (j != r, lambda l=l, j=j: tb_in(l, j).wait_recv()),
                (j == r, lambda l=l, j=j: tb_own(l, j).wait()),
            ])
        for q in range(ns):
            when_each([(q != s, lambda l=l, q=q: tc(l, q).start())])

    def gram_block(l, i, j):
        a = pl.ds(pl.multiple_of(i * 2 * tok, 2 * tok), 2 * tok)
        b = pl.ds(pl.multiple_of(j * 2 * tok, 2 * tok), 2 * tok)
        dims = (((1,), (1,)), ((), ()))
        x = lax.dot_general(c_all[l, a, :], c_all[l, b, :], dims, preferred_element_type=F32)
        ti = t_all[l, pl.ds(2 * i, 2)].reshape(2 * tok, ocols)
        tj = t_all[l, pl.ds(2 * j, 2)].reshape(2 * tok, ocols)
        y = lax.dot_general(ti, tj, dims, preferred_element_type=F32)
        p = x * y
        for da in range(2):
            part = jnp.sum(p[da * tok : (da + 1) * tok], axis=0, keepdims=True)
            for db in range(2):
                v = part[:, db * tok : db * tok + LANES]
                for e in range(1, tok // LANES):
                    v = v + part[:, db * tok + e * LANES : db * tok + (e + 1) * LANES]
                acc[l, 2 * i + da, pl.ds(2 * j + db, 1), :] = v
                acc[l, 2 * j + db, pl.ds(2 * i + da, 1), :] = v

    def gram_step(l, t):
        for way in range(2):
            when_each([(c_valid(way, t), lambda l=l, way=way, t=t: sib_in(l, c_in_chip(way, t)).wait_recv())])
        lo0, hi0 = jnp.maximum(z - t, 0), jnp.minimum(z + t, nz - 1)
        lo1, hi1 = jnp.maximum(z - 1 - t, 0), jnp.minimum(z + 1 + t, nz - 1)
        down = jnp.where(lo1 < lo0, hi0 - lo1 + 1, 0)
        up = jnp.where(hi1 > hi0, hi1 - lo1 + 1, 0)
        own = 1 if t == 0 else 0

        def body(k, _):
            i = jnp.where(k < own, z, jnp.where(k < own + down, lo1, lo1 + k - own - down))
            j = jnp.where(k < own, z, jnp.where(k < own + down, lo1 + k - own, hi1))
            gram_block(l, i, j)
            return 0

        lax.fori_loop(0, own + down + up, body, 0)

    def rows_sum_start(l):
        lane = lax.broadcasted_iota(jnp.int32, (n, LANES), 1)
        value = jnp.zeros((n, LANES), F32)
        for a in range(n):
            value = jnp.where(lane == a, jnp.sum(acc[l, a], axis=1, keepdims=True), value)
        ar1[l, s] = value
        mine[l, 0] = value
        for q in range(ns):
            when_each([(q != s, lambda q=q: remote(
                mine.at[l, 0], ar1.at[l, s], a1_send.at[l, q], a1_recv.at[l, s], r, q).start())])

    def replica_sum_start(l):
        for q in range(ns):
            when_each([(q != s, lambda q=q: remote(
                mine.at[l, 0], ar1.at[l, q], a1_send.at[l, q], a1_recv.at[l, q], r, q).wait_recv())])
        value = jnp.sum(ar1[l], axis=0)
        ar2[l, r] = value
        mine[l, 1] = value
        for j in range(n):
            when_each([(j != r, lambda j=j: remote(
                mine.at[l, 1], ar2.at[l, r], a2_send.at[l, j], a2_recv.at[l, r], j, s).start())])

    def gram_total(l):
        for j in range(n):
            when_each([(j != r, lambda j=j: remote(
                mine.at[l, 1], ar2.at[l, j], a2_send.at[l, j], a2_recv.at[l, j], j, s).wait_recv())])
        return jnp.sum(ar2[l], axis=0)

    def out_copy(l, m):
        part = pl.ds(pl.multiple_of(m * mt, mt), mt)
        return pltpu.make_async_copy(obuf.at[l, part], outs[l].at[part], osem.at[l, m])

    def finish(l):
        gram = gram_total(l) * (1.0 / (float(tok) * float(tok)))
        weights = replica_weights(gram, n) * (1.0 / float(tok))
        for rep in range(n):
            w = jnp.broadcast_to(weights[rep : rep + 1, :], (tok, ocols))
            t_scaled[rep * tok : (rep + 1) * tok, :] = (t_all[l, rep].astype(F32) * w).astype(jnp.bfloat16)

        def body(m, _):
            part = pl.ds(pl.multiple_of(m * mt, mt), mt)
            obuf[l, part, :] = lax.dot_general(
                c_all[l, :, part] if mt != cols else c_all[l],
                t_scaled[...], (((0,), (0,)), ((), ())), preferred_element_type=F32,
            )
            out_copy(l, m).start()
            return 0

        lax.fori_loop(0, cols // mt, body, 0)

    def inputs_ready(l):
        sib_in(l, z).wait_recv()
        for q in range(ns):
            when_each([(q != s, lambda q=q: tc_in(l, q).wait_recv())])

    last = nz - 2
    ta_start(0)
    own_start(0)
    ta_start(1)
    for copy in local:
        copy.wait()
    for l in layers:
        sib_out(l, z).start()
    tb_start(0)
    own_sent(0)
    own_start(1)
    arrive(0, 0)
    tb_start(1)
    share_t(0)
    for t in range(1, last):
        arrive(0, t)
        arrive(1, t - 1)
        if t == 1:
            share_t(1)
    inputs_ready(0)
    for t in range(last):
        gram_step(0, t)
    arrive(1, last - 1)
    arrive(0, last)
    gram_step(0, last)
    rows_sum_start(0)
    inputs_ready(1)
    gram_step(1, 0)
    replica_sum_start(0)
    for t in range(1, last):
        gram_step(1, t)
    finish(0)
    arrive(1, last)
    gram_step(1, last)
    rows_sum_start(1)
    replica_sum_start(1)
    finish(1)

    for l in layers:
        for q in range(ns):
            def drain(l=l, q=q):
                for h in range(2):
                    ta(l, q, h).wait_send()
                tc(l, q).wait_send()
                remote(mine.at[l, 0], ar1.at[l, s], a1_send.at[l, q], a1_recv.at[l, s], r, q).wait_send()

            when_each([(q != s, drain)])
        for j in range(n):
            def drain_b(l=l, j=j):
                tb(l, j).wait_send()
                remote(mine.at[l, 1], ar2.at[l, r], a2_send.at[l, j], a2_recv.at[l, r], j, s).wait_send()

            when_each([(j != r, drain_b)])
        sib_out(l, z).wait_send()
        for t in range(nz - 1):
            for way in range(2):
                when_each([
                    (jnp.logical_and(c_sends(way, t), l + t > 0), lambda l=l, way=way, t=t: c_copy(l, way, t).wait_send()),
                    (c_valid(way, t), lambda l=l, way=way, t=t: sib_out(l, c_in_chip(way, t)).wait_send()),
                ])
        for m in range(cols // mt):
            out_copy(l, m).wait()


def solution(mesh):
    n, ns = mesh.shape["replica"], mesh.shape["shard"]

    def shards(context_one, cotangent_one, context_two, cotangent_two):
        tok, cols = context_one.shape
        ocols = cols * ns // n
        mt = 256 if cols % 256 == 0 else cols
        nz = n // 2

        def halves(t):
            if ocols % LANES == 0:
                return t
            return t.reshape(tok, 2, ocols).transpose(1, 0, 2)

        dma = lambda *shape: pltpu.SemaphoreType.DMA(shape)
        bf = jnp.bfloat16
        any_spec = pl.BlockSpec(memory_space=pl.ANY)
        flops = LAYERS * 2 * n * tok * (cols * ocols + n * tok * (cols + ocols) // 2)
        return pl.pallas_call(
            functools.partial(kernel, n, ns, tok, cols, ocols, mt),
            out_shape=[jax.ShapeDtypeStruct((cols, ocols), F32)] * 2,
            in_specs=[any_spec] * 4,
            out_specs=[any_spec] * 2,
            scratch_shapes=[
                pltpu.VMEM((LAYERS, n * tok, cols), bf),
                pltpu.VMEM((LAYERS, n, tok, ocols), bf),
                pltpu.VMEM((LAYERS, ns, 2, tok // ns, ocols), bf),
                pltpu.VMEM((n * tok, ocols), bf),
                pltpu.VMEM((LAYERS, cols, ocols), F32),
                pltpu.VMEM((LAYERS, n, n, LANES), F32),
                pltpu.VMEM((LAYERS, ns, n, LANES), F32),
                pltpu.VMEM((LAYERS, n, n, LANES), F32),
                pltpu.VMEM((LAYERS, 2, n, LANES), F32),
                dma(LAYERS), dma(LAYERS, 2),
                dma(LAYERS, ns, 2), dma(LAYERS, ns, 2),
                dma(LAYERS), dma(LAYERS, n), dma(LAYERS, n),
                dma(LAYERS, ns), dma(LAYERS, ns),
                dma(LAYERS, 2, nz), dma(LAYERS, 2, nz),
                dma(LAYERS, nz), dma(LAYERS, nz),
                dma(LAYERS, ns), dma(LAYERS, ns),
                dma(LAYERS, n), dma(LAYERS, n),
                dma(LAYERS, cols // mt),
            ],
            compiler_params=pltpu.CompilerParams(
                collective_id=0, has_side_effects=True, vmem_limit_bytes=56 * 2**20
            ),
            cost_estimate=pl.CostEstimate(
                flops=flops, transcendentals=0,
                bytes_accessed=LAYERS * (2 * tok * cols * 2 + cols * ocols * 4),
            ),
        )(context_one, halves(cotangent_one), context_two, halves(cotangent_two))

    return jax.shard_map(
        shards,
        mesh=mesh,
        in_specs=(P("replica", "shard"),) * 4,
        out_specs=(P("shard", "replica"),) * 2,
        check_vma=False,
    )
```

```python
import functools

import jax
import jax.numpy as jnp
from jax import lax
from jax.experimental import pallas as pl
from jax.experimental.pallas import tpu as pltpu
from jax.sharding import PartitionSpec as P

EPSILON = 1e-06
MESH = pl.DeviceIdType.MESH
LAYERS = 2
LANES = 128
F32 = jnp.float32


def pair_coefficient(inner, own_sq, other_sq):
    own_sq = jnp.maximum(own_sq, 0.0)
    bound = jnp.sqrt(own_sq) * jnp.sqrt(jnp.maximum(other_sq, 0.0))
    inner = jnp.clip(inner, -bound, bound)
    return 1.0 - inner / (2.0 * (own_sq + EPSILON))


def replica_weights(gram, n):
    row = lax.broadcasted_iota(jnp.int32, gram.shape, 0)
    lane = lax.broadcasted_iota(jnp.int32, gram.shape, 1)
    col_w = jnp.ones((n, 1), F32)
    row_w = jnp.ones((1, LANES), F32)
    for level in range(n.bit_length() - 1):
        same = (row >> level) == (lane >> level)
        other = (row >> level) == ((lane >> level) ^ 1)
        scaled = gram * col_w * row_w
        inside = jnp.where(same, scaled, 0.0)
        across = jnp.where(other, scaled, 0.0)
        in_row = jnp.sum(inside, axis=0, keepdims=True)
        ac_row = jnp.sum(across, axis=0, keepdims=True)
        in_col = jnp.sum(inside, axis=1, keepdims=True)
        ac_col = jnp.sum(across, axis=1, keepdims=True)

        def total(mask, value, axis):
            return jnp.sum(jnp.where(mask, value, 0.0), axis=axis, keepdims=True)

        col_w = col_w * pair_coefficient(
            total(same, ac_row, 1), total(same, in_row, 1), total(other, in_row, 1)
        )
        row_w = row_w * pair_coefficient(
            total(same, ac_col, 0), total(same, in_col, 0), total(other, in_col, 0)
        )
    return col_w


def kernel(
    n, ns, tok, cols, ocols, mt,
    c1, t1, c2, t2, out1, out2,
    c_all, t_all, stage, t_scaled, obuf, acc, ar1, ar2, mine,
    loc_sem, tl_sem, ta_send, ta_recv, tb_loc, tb_send, tb_recv, tc_send, tc_recv, ts_send, ts_recv,
    c_send, c_recv, sib_send, sib_recv, a1_send, a1_recv, a2_send, a2_recv, osem,
):
    nz = n // 2
    tq = tok // ns
    c_in, t_in, outs = (c1, c2), (t1, t2), (out1, out2)
    r = lax.axis_index("replica")
    s = lax.axis_index("shard")
    z = r // 2
    core = r % 2
    sib = z * 2 + 1 - core
    layers = range(LAYERS)

    def remote(src, dst, ss, rs, dr, ds):
        return pltpu.make_async_remote_copy(
            src_ref=src, dst_ref=dst, send_sem=ss, recv_sem=rs,
            device_id=(dr, ds), device_id_type=MESH,
        )

    def rows(rep):
        return pl.ds(pl.multiple_of(rep * tok, tok), tok)

    def quarter(q):
        return pl.ds(pl.multiple_of(q * tq, tq), tq)

    def t_half(l, q, h):
        if ocols % LANES == 0:
            return t_in[l].at[quarter(q), pl.ds(h * ocols, ocols)]
        return t_in[l].at[h, quarter(q)]

    barrier = pltpu.get_barrier_semaphore()
    for q in range(ns):
        @pl.when(q != s)
        def _():
            pl.semaphore_signal(barrier, inc=1, device_id=(r, q), device_id_type=MESH)
    for rep in range(n):
        @pl.when(rep != r)
        def _():
            pl.semaphore_signal(barrier, inc=1, device_id=(rep, s), device_id_type=MESH)
    local = []
    for l in layers:
        local.append(pltpu.make_async_copy(c_in[l], c_all.at[l, rows(r)], loc_sem.at[l]))
        for h in range(2):
            local.append(pltpu.make_async_copy(t_half(l, s, h), stage.at[l, s, h], tl_sem.at[l, h]))
    for copy in local:
        copy.start()
    pl.semaphore_wait(barrier, n + ns - 2)

    def ta(l, q, h):
        return remote(t_half(l, q, h), stage.at[l, s, h], ta_send.at[l, q, h],
                      ta_recv.at[l, s, h], r, q)

    def ta_in(l, q, h):
        return remote(t_half(l, s, h), stage.at[l, q, h], ta_send.at[l, q, h],
                      ta_recv.at[l, q, h], r, q)

    def tb(l, j):
        return remote(stage.at[l, j // 2, j % 2], t_all.at[l, 0, r, quarter(s)],
                      tb_send.at[l, j], tb_recv.at[l, r], j, s)

    def tb_in(l, j):
        return remote(stage.at[l, j // 2, j % 2], t_all.at[l, 0, j, quarter(s)],
                      tb_send.at[l, j], tb_recv.at[l, j], j, s)

    def tb_own(l, j):
        return pltpu.make_async_copy(stage.at[l, j // 2, j % 2], t_all.at[l, 0, r, quarter(s)], tb_loc.at[l])

    def tc(l, q):
        part = t_all.at[l, 0, :, quarter(s)]
        return remote(part, part, tc_send.at[l, q], tc_recv.at[l, s], r, q)

    def tc_in(l, q):
        part = t_all.at[l, 0, :, quarter(q)]
        return remote(part, part, tc_send.at[l, q], tc_recv.at[l, q], r, q)

    def t_sib(l):
        return remote(t_all.at[l, 0], t_all.at[l, 1], ts_send.at[l], ts_recv.at[l], sib, s)

    def c_copy(l, way, t):
        chip = z - t if way == 0 else z + t
        block = c_all.at[l, rows(2 * chip + core)]
        src = c_in[l] if t == 0 else block
        to = r + 2 if way == 0 else r - 2
        return remote(src, block, c_send.at[l, way, t], c_recv.at[l, way, t], to, s)

    def c_sends(way, t):
        if way == 0:
            return jnp.logical_and(z < nz - 1, z - t >= 0)
        return jnp.logical_and(z > 0, z + t <= nz - 1)

    def c_in_chip(way, t):
        return z - 1 - t if way == 0 else z + 1 + t

    def c_valid(way, t):
        chip = c_in_chip(way, t)
        return chip >= 0 if way == 0 else chip <= nz - 1

    def c_wait(l, way, t):
        block = c_all.at[l, rows(2 * c_in_chip(way, t) + core)]
        remote(block, block, c_send.at[l, way, t], c_recv.at[l, way, t], sib, s).wait_recv()

    def sib_out(l, chip):
        block = c_all.at[l, rows(2 * chip + core)]
        return remote(block, block, sib_send.at[l, chip], sib_recv.at[l, chip], sib, s)

    def sib_in(l, chip):
        block = c_all.at[l, rows(2 * chip + 1 - core)]
        return remote(block, block, sib_send.at[l, chip], sib_recv.at[l, chip], sib, s)

    def when_each(pairs):
        for cond, fn in pairs:
            pl.when(cond)(fn)

    def ta_start(l):
        for q in range(ns):
            for h in range(2):
                when_each([(q != s, lambda q=q, h=h: ta(l, q, h).start())])

    def own_start(l):
        for way in range(2):
            when_each([(c_sends(way, 0), lambda way=way: c_copy(l, way, 0).start())])

    def own_sent(l):
        for way in range(2):
            when_each([(c_sends(way, 0), lambda way=way: c_copy(l, way, 0).wait_send())])

    def tb_start(l):
        for q in range(ns):
            for h in range(2):
                when_each([(q != s, lambda q=q, h=h: ta_in(l, q, h).wait_recv())])
        for j in range(n):
            when_each([
                (j != r, lambda j=j: tb(l, j).start()),
                (j == r, lambda j=j: tb_own(l, j).start()),
            ])

    def arrive(l, t):
        for way in range(2):
            def take(l=l, way=way, t=t):
                c_wait(l, way, t)
                if t + 1 <= nz - 2:
                    when_each([(c_sends(way, t + 1), lambda: c_copy(l, way, t + 1).start())])
                sib_out(l, c_in_chip(way, t)).start()

            when_each([(c_valid(way, t), take)])

    def share_t(l):
        for j in range(n):
            when_each([
                (j != r, lambda l=l, j=j: tb_in(l, j).wait_recv()),
                (j == r, lambda l=l, j=j: tb_own(l, j).wait()),
            ])
        for q in range(ns):
            when_each([(q != s, lambda l=l, q=q: tc(l, q).start())])

    def gram_block(l, i, chip):
        b = 2 * chip + core
        pair = pl.ds(pl.multiple_of(i * 2 * tok, 2 * tok), 2 * tok)
        dims = (((1,), (1,)), ((), ()))
        x = lax.dot_general(c_all[l, pair, :], c_all[l, rows(b), :], dims, preferred_element_type=F32)
        y = jnp.zeros_like(x)
        for h in range(2):
            ti = t_all[l, h, pl.ds(2 * i, 2)].reshape(2 * tok, ocols)
            y = y + lax.dot_general(ti, t_all[l, h, b], dims, preferred_element_type=F32)
        p = x * y
        for da in range(2):
            a = 2 * i + da
            share = jnp.where(jnp.logical_and(i == chip, a != b), 0.5, 1.0)
            part = jnp.sum(p[da * tok : (da + 1) * tok], axis=0, keepdims=True)
            v = part[:, :LANES]
            for e in range(1, tok // LANES):
                v = v + part[:, e * LANES : (e + 1) * LANES]
            v = v * share
            acc[l, a, pl.ds(b, 1), :] = v
            acc[l, b, pl.ds(a, 1), :] = v

    def gram_step(l, t):
        lo0, hi0 = jnp.maximum(z - t, 0), jnp.minimum(z + t, nz - 1)
        lo1, hi1 = jnp.maximum(z - 1 - t, 0), jnp.minimum(z + 1 + t, nz - 1)
        down = jnp.where(lo1 < lo0, 1, 0)
        up = jnp.where(hi1 > hi0, 1, 0)
        width = hi0 - lo0 + 1
        own = 1 if t == 0 else 0

        def earlier(k, _):
            first = k < down * width
            gram_block(l, jnp.where(first, lo0 + k, lo0 + k - down * width), jnp.where(first, lo1, hi1))
            return 0

        def among(k, _):
            i = jnp.where(k < own, z, jnp.where(k < own + down, lo1, jnp.where(k < own + down + up, hi1, lo1)))
            chip = jnp.where(k < own, z, jnp.where(k < own + down, lo1, hi1))
            gram_block(l, i, chip)
            return 0

        lax.fori_loop(0, (down + up) * width, earlier, 0)
        for way in range(2):
            when_each([(c_valid(way, t), lambda way=way: sib_in(l, c_in_chip(way, t)).wait_recv())])
        lax.fori_loop(0, own + down + up + down * up, among, 0)

    def rows_sum_start(l):
        lane = lax.broadcasted_iota(jnp.int32, (n, LANES), 1)
        value = jnp.zeros((n, LANES), F32)
        for a in range(n):
            value = jnp.where(lane == a, jnp.sum(acc[l, a], axis=1, keepdims=True), value)
        ar1[l, s] = value
        mine[l, 0] = value
        for q in range(ns):
            when_each([(q != s, lambda q=q: remote(
                mine.at[l, 0], ar1.at[l, s], a1_send.at[l, q], a1_recv.at[l, s], r, q).start())])

    def replica_sum_start(l):
        for q in range(ns):
            when_each([(q != s, lambda q=q: remote(
                mine.at[l, 0], ar1.at[l, q], a1_send.at[l, q], a1_recv.at[l, q], r, q).wait_recv())])
        value = jnp.sum(ar1[l], axis=0)
        ar2[l, r] = value
        mine[l, 1] = value
        for j in range(n):
            when_each([(j != r, lambda j=j: remote(
                mine.at[l, 1], ar2.at[l, r], a2_send.at[l, j], a2_recv.at[l, r], j, s).start())])

    def gram_total(l):
        for j in range(n):
            when_each([(j != r, lambda j=j: remote(
                mine.at[l, 1], ar2.at[l, j], a2_send.at[l, j], a2_recv.at[l, j], j, s).wait_recv())])
        return jnp.sum(ar2[l], axis=0)

    def out_copy(l, m):
        part = pl.ds(pl.multiple_of(m * mt, mt), mt)
        return pltpu.make_async_copy(obuf.at[l, part], outs[l].at[part], osem.at[l, m])

    def finish(l):
        gram = gram_total(l) * (1.0 / (float(tok) * float(tok)))
        weights = replica_weights(gram, n) * (1.0 / float(tok))
        for rep in range(n):
            w = jnp.broadcast_to(weights[rep : rep + 1, :], (tok, ocols))
            t_scaled[rep * tok : (rep + 1) * tok, :] = (t_all[l, 0, rep].astype(F32) * w).astype(jnp.bfloat16)

        def body(m, _):
            part = pl.ds(pl.multiple_of(m * mt, mt), mt)
            obuf[l, part, :] = lax.dot_general(
                c_all[l, :, part] if mt != cols else c_all[l],
                t_scaled[...], (((0,), (0,)), ((), ())), preferred_element_type=F32,
            ).astype(jnp.bfloat16)
            out_copy(l, m).start()
            return 0

        lax.fori_loop(0, cols // mt, body, 0)

    def inputs_ready(l):
        for q in range(ns):
            when_each([(q != s, lambda q=q: tc_in(l, q).wait_recv())])
        t_sib(l).start()
        sib_in(l, z).wait_recv()
        t_sib(l).wait_recv()

    last = nz - 2
    at_end = jnp.logical_or(z == 0, z == nz - 1)
    ta_start(0)
    own_start(0)
    acc[...] = jnp.zeros_like(acc)
    for copy in local:
        copy.wait()
    for l in layers:
        sib_out(l, z).start()
    tb_start(0)
    ta_start(1)
    tb_start(1)
    own_sent(0)
    own_start(1)
    arrive(0, 0)
    share_t(0)
    share_t(1)
    for t in range(1, last):
        arrive(0, t)
        arrive(1, t - 1)
    when_each([(jnp.logical_not(at_end), lambda: arrive(1, last - 1))])
    inputs_ready(0)
    for t in range(last):
        gram_step(0, t)
    arrive(0, last)
    gram_step(0, last)
    rows_sum_start(0)
    inputs_ready(1)
    gram_step(1, 0)
    replica_sum_start(0)
    when_each([(at_end, lambda: arrive(1, last - 1))])
    for t in range(1, last):
        gram_step(1, t)
    finish(0)
    arrive(1, last)
    gram_step(1, last)
    rows_sum_start(1)
    replica_sum_start(1)
    finish(1)

    for l in layers:
        for q in range(ns):
            def drain(l=l, q=q):
                for h in range(2):
                    ta(l, q, h).wait_send()
                tc(l, q).wait_send()
                remote(mine.at[l, 0], ar1.at[l, s], a1_send.at[l, q], a1_recv.at[l, s], r, q).wait_send()

            when_each([(q != s, drain)])
        for j in range(n):
            def drain_b(l=l, j=j):
                tb(l, j).wait_send()
                remote(mine.at[l, 1], ar2.at[l, r], a2_send.at[l, j], a2_recv.at[l, r], j, s).wait_send()

            when_each([(j != r, drain_b)])
        sib_out(l, z).wait_send()
        t_sib(l).wait_send()
        for t in range(nz - 1):
            for way in range(2):
                when_each([
                    (jnp.logical_and(c_sends(way, t), l + t > 0), lambda l=l, way=way, t=t: c_copy(l, way, t).wait_send()),
                    (c_valid(way, t), lambda l=l, way=way, t=t: sib_out(l, c_in_chip(way, t)).wait_send()),
                ])
        for m in range(cols // mt):
            out_copy(l, m).wait()


def solution(mesh):
    n, ns = mesh.shape["replica"], mesh.shape["shard"]

    def shards(context_one, cotangent_one, context_two, cotangent_two):
        tok, cols = context_one.shape
        ocols = cols * ns // n
        mt = 256 if cols % 256 == 0 else cols
        nz = n // 2

        def halves(t):
            if ocols % LANES == 0:
                return t
            return t.reshape(tok, 2, ocols).transpose(1, 0, 2)

        dma = lambda *shape: pltpu.SemaphoreType.DMA(shape)
        bf = jnp.bfloat16
        any_spec = pl.BlockSpec(memory_space=pl.ANY)
        flops = LAYERS * 2 * n * tok * (cols * ocols + n * tok * (cols + ocols) // 2)
        combined = pl.pallas_call(
            functools.partial(kernel, n, ns, tok, cols, ocols, mt),
            out_shape=[jax.ShapeDtypeStruct((cols, ocols), bf)] * 2,
            in_specs=[any_spec] * 4,
            out_specs=[any_spec] * 2,
            scratch_shapes=[
                pltpu.VMEM((LAYERS, n * tok, cols), bf),
                pltpu.VMEM((LAYERS, 2, n, tok, ocols), bf),
                pltpu.VMEM((LAYERS, ns, 2, tok // ns, ocols), bf),
                pltpu.VMEM((n * tok, ocols), bf),
                pltpu.VMEM((LAYERS, cols, ocols), bf),
                pltpu.VMEM((LAYERS, n, n, LANES), F32),
                pltpu.VMEM((LAYERS, ns, n, LANES), F32),
                pltpu.VMEM((LAYERS, n, n, LANES), F32),
                pltpu.VMEM((LAYERS, 2, n, LANES), F32),
                dma(LAYERS), dma(LAYERS, 2),
                dma(LAYERS, ns, 2), dma(LAYERS, ns, 2),
                dma(LAYERS), dma(LAYERS, n), dma(LAYERS, n),
                dma(LAYERS, ns), dma(LAYERS, ns), dma(LAYERS), dma(LAYERS),
                dma(LAYERS, 2, nz), dma(LAYERS, 2, nz),
                dma(LAYERS, nz), dma(LAYERS, nz),
                dma(LAYERS, ns), dma(LAYERS, ns),
                dma(LAYERS, n), dma(LAYERS, n),
                dma(LAYERS, cols // mt),
            ],
            compiler_params=pltpu.CompilerParams(
                collective_id=0, has_side_effects=True, vmem_limit_bytes=56 * 2**20
            ),
            cost_estimate=pl.CostEstimate(
                flops=flops, transcendentals=0,
                bytes_accessed=LAYERS * (2 * tok * cols * 2 + cols * ocols * 2),
            ),
        )(context_one, halves(cotangent_one), context_two, halves(cotangent_two))
        return tuple(value.astype(F32) for value in combined)

    return jax.shard_map(
        shards,
        mesh=mesh,
        in_specs=(P("replica", "shard"),) * 4,
        out_specs=(P("shard", "replica"),) * 2,
        check_vma=False,
    )
```

```python
import functools

import jax
import jax.numpy as jnp
from jax import lax
from jax.experimental import pallas as pl
from jax.experimental.pallas import tpu as pltpu
from jax.sharding import PartitionSpec as P

EPSILON = 1e-06
MESH = pl.DeviceIdType.MESH
LAYERS = 2
LANES = 128
F32 = jnp.float32


def pair_coefficient(inner, own_sq, other_sq):
    own_sq = jnp.maximum(own_sq, 0.0)
    bound = jnp.sqrt(own_sq) * jnp.sqrt(jnp.maximum(other_sq, 0.0))
    inner = jnp.clip(inner, -bound, bound)
    return 1.0 - inner / (2.0 * (own_sq + EPSILON))


def replica_weights(gram, n):
    row = lax.broadcasted_iota(jnp.int32, gram.shape, 0)
    lane = lax.broadcasted_iota(jnp.int32, gram.shape, 1)
    col_w = jnp.ones((n, 1), F32)
    row_w = jnp.ones((1, LANES), F32)
    for level in range(n.bit_length() - 1):
        same = (row >> level) == (lane >> level)
        other = (row >> level) == ((lane >> level) ^ 1)
        scaled = gram * col_w * row_w
        inside = jnp.where(same, scaled, 0.0)
        across = jnp.where(other, scaled, 0.0)
        in_row = jnp.sum(inside, axis=0, keepdims=True)
        ac_row = jnp.sum(across, axis=0, keepdims=True)
        in_col = jnp.sum(inside, axis=1, keepdims=True)
        ac_col = jnp.sum(across, axis=1, keepdims=True)

        def total(mask, value, axis):
            return jnp.sum(jnp.where(mask, value, 0.0), axis=axis, keepdims=True)

        col_w = col_w * pair_coefficient(
            total(same, ac_row, 1), total(same, in_row, 1), total(other, in_row, 1)
        )
        row_w = row_w * pair_coefficient(
            total(same, ac_col, 0), total(same, in_col, 0), total(other, in_col, 0)
        )
    return col_w


def kernel(
    n, ns, tok, cols, ocols, mt,
    c1, t1, c2, t2, out1, out2,
    c_all, t_all, stage, t_scaled, obuf, acc, ar1, ar2, mine,
    loc_sem, tl_sem, ta_send, ta_recv, tb_loc, tb_send, tb_recv, tc_send, tc_recv, ts_send, ts_recv,
    c_send, c_recv, sib_send, sib_recv, a1_send, a1_recv, a2_send, a2_recv, osem,
):
    nz = n // 2
    tq = tok // ns
    c_in, t_in, outs = (c1, c2), (t1, t2), (out1, out2)
    r = lax.axis_index("replica")
    s = lax.axis_index("shard")
    z = r // 2
    core = r % 2
    sib = z * 2 + 1 - core
    layers = range(LAYERS)

    def remote(src, dst, ss, rs, dr, ds):
        return pltpu.make_async_remote_copy(
            src_ref=src, dst_ref=dst, send_sem=ss, recv_sem=rs,
            device_id=(dr, ds), device_id_type=MESH,
        )

    def rows(rep):
        return pl.ds(pl.multiple_of(rep * tok, tok), tok)

    def quarter(q):
        return pl.ds(pl.multiple_of(q * tq, tq), tq)

    def t_half(l, q, h):
        if ocols % LANES == 0:
            return t_in[l].at[quarter(q), pl.ds(h * ocols, ocols)]
        return t_in[l].at[h, quarter(q)]

    barrier = pltpu.get_barrier_semaphore()
    for q in range(ns):
        @pl.when(q != s)
        def _():
            pl.semaphore_signal(barrier, inc=1, device_id=(r, q), device_id_type=MESH)
    for rep in range(n):
        @pl.when(rep != r)
        def _():
            pl.semaphore_signal(barrier, inc=1, device_id=(rep, s), device_id_type=MESH)
    local = []
    for l in layers:
        local.append(pltpu.make_async_copy(c_in[l], c_all.at[l, rows(r)], loc_sem.at[l]))
        for h in range(2):
            local.append(pltpu.make_async_copy(t_half(l, s, h), stage.at[l, s, h], tl_sem.at[l, h]))
    for copy in local:
        copy.start()
    pl.semaphore_wait(barrier, n + ns - 2)

    def ta(l, q, h):
        return remote(t_half(l, q, h), stage.at[l, s, h], ta_send.at[l, q, h],
                      ta_recv.at[l, s, h], r, q)

    def ta_in(l, q, h):
        return remote(t_half(l, s, h), stage.at[l, q, h], ta_send.at[l, q, h],
                      ta_recv.at[l, q, h], r, q)

    def tb(l, j):
        return remote(stage.at[l, j // 2, j % 2], t_all.at[l, 0, r, quarter(s)],
                      tb_send.at[l, j], tb_recv.at[l, r], j, s)

    def tb_in(l, j):
        return remote(stage.at[l, j // 2, j % 2], t_all.at[l, 0, j, quarter(s)],
                      tb_send.at[l, j], tb_recv.at[l, j], j, s)

    def tb_own(l, j):
        return pltpu.make_async_copy(stage.at[l, j // 2, j % 2], t_all.at[l, 0, r, quarter(s)], tb_loc.at[l])

    def tc(l, q, chip):
        part = t_all.at[l, 0, pl.ds(2 * chip, 2), quarter(s)]
        return remote(part, part, tc_send.at[l, q, chip], tc_recv.at[l, s, chip], r, q)

    def tc_in(l, q, chip):
        part = t_all.at[l, 0, pl.ds(2 * chip, 2), quarter(q)]
        return remote(part, part, tc_send.at[l, q, chip], tc_recv.at[l, q, chip], r, q)

    def t_sib(l, q):
        return remote(t_all.at[l, 0, :, quarter(q)], t_all.at[l, 1, :, quarter(q)],
                      ts_send.at[l, q], ts_recv.at[l, q], sib, s)

    def c_copy(l, way, t):
        chip = z - t if way == 0 else z + t
        block = c_all.at[l, rows(2 * chip + core)]
        src = c_in[l] if t == 0 else block
        to = r + 2 if way == 0 else r - 2
        return remote(src, block, c_send.at[l, way, t], c_recv.at[l, way, t], to, s)

    def c_sends(way, t):
        if way == 0:
            return jnp.logical_and(z < nz - 1, z - t >= 0)
        return jnp.logical_and(z > 0, z + t <= nz - 1)

    def c_in_chip(way, t):
        return z - 1 - t if way == 0 else z + 1 + t

    def c_valid(way, t):
        chip = c_in_chip(way, t)
        return chip >= 0 if way == 0 else chip <= nz - 1

    def c_wait(l, way, t):
        block = c_all.at[l, rows(2 * c_in_chip(way, t) + core)]
        remote(block, block, c_send.at[l, way, t], c_recv.at[l, way, t], sib, s).wait_recv()

    def sib_out(l, chip):
        block = c_all.at[l, rows(2 * chip + core)]
        return remote(block, block, sib_send.at[l, chip], sib_recv.at[l, chip], sib, s)

    def sib_in(l, chip):
        block = c_all.at[l, rows(2 * chip + 1 - core)]
        return remote(block, block, sib_send.at[l, chip], sib_recv.at[l, chip], sib, s)

    def when_each(pairs):
        for cond, fn in pairs:
            pl.when(cond)(fn)

    def ta_start(l):
        for q in range(ns):
            for h in range(2):
                when_each([(q != s, lambda q=q, h=h: ta(l, q, h).start())])

    def own_start(l):
        for way in range(2):
            when_each([(c_sends(way, 0), lambda way=way: c_copy(l, way, 0).start())])

    def own_sent(l):
        for way in range(2):
            when_each([(c_sends(way, 0), lambda way=way: c_copy(l, way, 0).wait_send())])

    def tb_start(l):
        for q in range(ns):
            for h in range(2):
                when_each([(q != s, lambda q=q, h=h: ta_in(l, q, h).wait_recv())])
        for j in range(n):
            when_each([
                (j != r, lambda j=j: tb(l, j).start()),
                (j == r, lambda j=j: tb_own(l, j).start()),
            ])

    def arrive(l, t):
        for way in range(2):
            def take(l=l, way=way, t=t):
                c_wait(l, way, t)
                if t + 1 <= nz - 2:
                    when_each([(c_sends(way, t + 1), lambda: c_copy(l, way, t + 1).start())])
                sib_out(l, c_in_chip(way, t)).start()

            when_each([(c_valid(way, t), take)])

    def share_t(l):
        for k in range(nz):
            chip = lax.rem(z + k, nz)
            if k == 0:
                tb_own(l, r).wait()
                tb_in(l, sib).wait_recv()
            else:
                tb_in(l, 2 * chip).wait_recv()
                tb_in(l, 2 * chip + 1).wait_recv()
            for q in range(ns):
                when_each([(q != s, lambda q=q, chip=chip: tc(l, q, chip).start())])
        t_sib(l, s).start()

    def gram_block(l, i, chip):
        b = 2 * chip + core
        pair = pl.ds(pl.multiple_of(i * 2 * tok, 2 * tok), 2 * tok)
        dims = (((1,), (1,)), ((), ()))
        x = lax.dot_general(c_all[l, pair, :], c_all[l, rows(b), :], dims, preferred_element_type=F32)
        y = jnp.zeros_like(x)
        for h in range(2):
            ti = t_all[l, h, pl.ds(2 * i, 2)].reshape(2 * tok, ocols)
            y = y + lax.dot_general(ti, t_all[l, h, b], dims, preferred_element_type=F32)
        p = x * y
        for da in range(2):
            a = 2 * i + da
            share = jnp.where(jnp.logical_and(i == chip, a != b), 0.5, 1.0)
            part = jnp.sum(p[da * tok : (da + 1) * tok], axis=0, keepdims=True)
            v = part[:, :LANES]
            for e in range(1, tok // LANES):
                v = v + part[:, e * LANES : (e + 1) * LANES]
            v = v * share
            acc[l, a, pl.ds(b, 1), :] = v
            acc[l, b, pl.ds(a, 1), :] = v

    def gram_step(l, t):
        lo0, hi0 = jnp.maximum(z - t, 0), jnp.minimum(z + t, nz - 1)
        lo1, hi1 = jnp.maximum(z - 1 - t, 0), jnp.minimum(z + 1 + t, nz - 1)
        down = jnp.where(lo1 < lo0, 1, 0)
        up = jnp.where(hi1 > hi0, 1, 0)
        width = hi0 - lo0 + 1
        own = 1 if t == 0 else 0

        def earlier(k, _):
            first = k < down * width
            gram_block(l, jnp.where(first, lo0 + k, lo0 + k - down * width), jnp.where(first, lo1, hi1))
            return 0

        def among(k, _):
            i = jnp.where(k < own, z, jnp.where(k < own + down, lo1, jnp.where(k < own + down + up, hi1, lo1)))
            chip = jnp.where(k < own, z, jnp.where(k < own + down, lo1, hi1))
            gram_block(l, i, chip)
            return 0

        lax.fori_loop(0, (down + up) * width, earlier, 0)
        for way in range(2):
            when_each([(c_valid(way, t), lambda way=way: sib_in(l, c_in_chip(way, t)).wait_recv())])
        lax.fori_loop(0, own + down + up + down * up, among, 0)

    def rows_sum_start(l):
        lane = lax.broadcasted_iota(jnp.int32, (n, LANES), 1)
        value = jnp.zeros((n, LANES), F32)
        for a in range(n):
            value = jnp.where(lane == a, jnp.sum(acc[l, a], axis=1, keepdims=True), value)
        ar1[l, s] = value
        mine[l, 0] = value
        for q in range(ns):
            when_each([(q != s, lambda q=q: remote(
                mine.at[l, 0], ar1.at[l, s], a1_send.at[l, q], a1_recv.at[l, s], r, q).start())])

    def replica_sum_start(l):
        for q in range(ns):
            when_each([(q != s, lambda q=q: remote(
                mine.at[l, 0], ar1.at[l, q], a1_send.at[l, q], a1_recv.at[l, q], r, q).wait_recv())])
        value = jnp.sum(ar1[l], axis=0)
        ar2[l, r] = value
        mine[l, 1] = value
        for j in range(n):
            when_each([(j != r, lambda j=j: remote(
                mine.at[l, 1], ar2.at[l, r], a2_send.at[l, j], a2_recv.at[l, r], j, s).start())])

    def gram_total(l):
        for j in range(n):
            when_each([(j != r, lambda j=j: remote(
                mine.at[l, 1], ar2.at[l, j], a2_send.at[l, j], a2_recv.at[l, j], j, s).wait_recv())])
        return jnp.sum(ar2[l], axis=0)

    def out_copy(l, m):
        part = pl.ds(pl.multiple_of(m * mt, mt), mt)
        return pltpu.make_async_copy(obuf.at[l, part], outs[l].at[part], osem.at[l, m])

    def finish(l):
        gram = gram_total(l) * (1.0 / (float(tok) * float(tok)))
        weights = replica_weights(gram, n) * (1.0 / float(tok))
        for rep in range(n):
            w = jnp.broadcast_to(weights[rep : rep + 1, :], (tok, ocols))
            t_scaled[rep * tok : (rep + 1) * tok, :] = (t_all[l, 0, rep].astype(F32) * w).astype(jnp.bfloat16)

        def body(m, _):
            part = pl.ds(pl.multiple_of(m * mt, mt), mt)
            obuf[l, part, :] = lax.dot_general(
                c_all[l, :, part] if mt != cols else c_all[l],
                t_scaled[...], (((0,), (0,)), ((), ())), preferred_element_type=F32,
            ).astype(jnp.bfloat16)
            out_copy(l, m).start()
            return 0

        lax.fori_loop(0, cols // mt, body, 0)

    def inputs_ready(l):
        for q in range(ns):
            def pass_on(q=q):
                for chip in range(nz):
                    tc_in(l, q, chip).wait_recv()
                t_sib(l, q).start()

            when_each([(q != s, pass_on)])
        sib_in(l, z).wait_recv()
        for q in range(ns):
            t_sib(l, q).wait_recv()

    last = nz - 2
    at_end = jnp.logical_or(z == 0, z == nz - 1)
    ta_start(0)
    own_start(0)
    acc[...] = jnp.zeros_like(acc)
    for copy in local:
        copy.wait()
    for l in layers:
        sib_out(l, z).start()
    tb_start(0)
    ta_start(1)
    share_t(0)
    tb_start(1)
    own_sent(0)
    own_start(1)
    arrive(0, 0)
    share_t(1)
    for t in range(1, last):
        arrive(0, t)
        arrive(1, t - 1)
    when_each([(jnp.logical_not(at_end), lambda: arrive(1, last - 1))])
    inputs_ready(0)
    for t in range(last):
        gram_step(0, t)
    arrive(0, last)
    gram_step(0, last)
    rows_sum_start(0)
    inputs_ready(1)
    gram_step(1, 0)
    replica_sum_start(0)
    when_each([(at_end, lambda: arrive(1, last - 1))])
    for t in range(1, last):
        gram_step(1, t)
    finish(0)
    arrive(1, last)
    gram_step(1, last)
    rows_sum_start(1)
    replica_sum_start(1)
    finish(1)

    for l in layers:
        for q in range(ns):
            def drain(l=l, q=q):
                for h in range(2):
                    ta(l, q, h).wait_send()
                for chip in range(nz):
                    tc(l, q, chip).wait_send()
                remote(mine.at[l, 0], ar1.at[l, s], a1_send.at[l, q], a1_recv.at[l, s], r, q).wait_send()

            when_each([(q != s, drain)])
        for j in range(n):
            def drain_b(l=l, j=j):
                tb(l, j).wait_send()
                remote(mine.at[l, 1], ar2.at[l, r], a2_send.at[l, j], a2_recv.at[l, r], j, s).wait_send()

            when_each([(j != r, drain_b)])
        sib_out(l, z).wait_send()
        for q in range(ns):
            t_sib(l, q).wait_send()
        for t in range(nz - 1):
            for way in range(2):
                when_each([
                    (jnp.logical_and(c_sends(way, t), l + t > 0), lambda l=l, way=way, t=t: c_copy(l, way, t).wait_send()),
                    (c_valid(way, t), lambda l=l, way=way, t=t: sib_out(l, c_in_chip(way, t)).wait_send()),
                ])
        for m in range(cols // mt):
            out_copy(l, m).wait()


def solution(mesh):
    n, ns = mesh.shape["replica"], mesh.shape["shard"]

    def shards(context_one, cotangent_one, context_two, cotangent_two):
        tok, cols = context_one.shape
        ocols = cols * ns // n
        mt = 256 if cols % 256 == 0 else cols
        nz = n // 2

        def halves(t):
            if ocols % LANES == 0:
                return t
            return t.reshape(tok, 2, ocols).transpose(1, 0, 2)

        dma = lambda *shape: pltpu.SemaphoreType.DMA(shape)
        bf = jnp.bfloat16
        any_spec = pl.BlockSpec(memory_space=pl.ANY)
        flops = LAYERS * 2 * n * tok * (cols * ocols + n * tok * (cols + ocols) // 2)
        combined = pl.pallas_call(
            functools.partial(kernel, n, ns, tok, cols, ocols, mt),
            out_shape=[jax.ShapeDtypeStruct((cols, ocols), bf)] * 2,
            in_specs=[any_spec] * 4,
            out_specs=[any_spec] * 2,
            scratch_shapes=[
                pltpu.VMEM((LAYERS, n * tok, cols), bf),
                pltpu.VMEM((LAYERS, 2, n, tok, ocols), bf),
                pltpu.VMEM((LAYERS, ns, 2, tok // ns, ocols), bf),
                pltpu.VMEM((n * tok, ocols), bf),
                pltpu.VMEM((LAYERS, cols, ocols), bf),
                pltpu.VMEM((LAYERS, n, n, LANES), F32),
                pltpu.VMEM((LAYERS, ns, n, LANES), F32),
                pltpu.VMEM((LAYERS, n, n, LANES), F32),
                pltpu.VMEM((LAYERS, 2, n, LANES), F32),
                dma(LAYERS), dma(LAYERS, 2),
                dma(LAYERS, ns, 2), dma(LAYERS, ns, 2),
                dma(LAYERS), dma(LAYERS, n), dma(LAYERS, n),
                dma(LAYERS, ns, nz), dma(LAYERS, ns, nz), dma(LAYERS, ns), dma(LAYERS, ns),
                dma(LAYERS, 2, nz), dma(LAYERS, 2, nz),
                dma(LAYERS, nz), dma(LAYERS, nz),
                dma(LAYERS, ns), dma(LAYERS, ns),
                dma(LAYERS, n), dma(LAYERS, n),
                dma(LAYERS, cols // mt),
            ],
            compiler_params=pltpu.CompilerParams(
                collective_id=0, has_side_effects=True, vmem_limit_bytes=56 * 2**20
            ),
            cost_estimate=pl.CostEstimate(
                flops=flops, transcendentals=0,
                bytes_accessed=LAYERS * (2 * tok * cols * 2 + cols * ocols * 2),
            ),
        )(context_one, halves(cotangent_one), context_two, halves(cotangent_two))
        return tuple(value.astype(F32) for value in combined)

    return jax.shard_map(
        shards,
        mesh=mesh,
        in_specs=(P("replica", "shard"),) * 4,
        out_specs=(P("shard", "replica"),) * 2,
        check_vma=False,
    )
```

```python
import functools

import jax
import jax.numpy as jnp
from jax import lax
from jax.experimental import pallas as pl
from jax.experimental.pallas import tpu as pltpu
from jax.sharding import PartitionSpec as P

EPSILON = 1e-06
MESH = pl.DeviceIdType.MESH
LAYERS = 2
LANES = 128
F32 = jnp.float32


def pair_coefficient(inner, own_sq, other_sq):
    own_sq = jnp.maximum(own_sq, 0.0)
    bound = jnp.sqrt(own_sq) * jnp.sqrt(jnp.maximum(other_sq, 0.0))
    inner = jnp.clip(inner, -bound, bound)
    return 1.0 - inner / (2.0 * (own_sq + EPSILON))


def replica_weights(gram, n):
    row = lax.broadcasted_iota(jnp.int32, gram.shape, 0)
    lane = lax.broadcasted_iota(jnp.int32, gram.shape, 1)
    col_w = jnp.ones((n, 1), F32)
    row_w = jnp.ones((1, LANES), F32)
    for level in range(n.bit_length() - 1):
        same = (row >> level) == (lane >> level)
        other = (row >> level) == ((lane >> level) ^ 1)
        scaled = gram * col_w * row_w
        inside = jnp.where(same, scaled, 0.0)
        across = jnp.where(other, scaled, 0.0)
        in_row = jnp.sum(inside, axis=0, keepdims=True)
        ac_row = jnp.sum(across, axis=0, keepdims=True)
        in_col = jnp.sum(inside, axis=1, keepdims=True)
        ac_col = jnp.sum(across, axis=1, keepdims=True)

        def total(mask, value, axis):
            return jnp.sum(jnp.where(mask, value, 0.0), axis=axis, keepdims=True)

        col_w = col_w * pair_coefficient(
            total(same, ac_row, 1), total(same, in_row, 1), total(other, in_row, 1)
        )
        row_w = row_w * pair_coefficient(
            total(same, ac_col, 0), total(same, in_col, 0), total(other, in_col, 0)
        )
    return col_w


def kernel(
    n, ns, tok, cols, ocols, mt,
    c1, t1, c2, t2, out1, out2,
    c_all, ct_all, t_all, stage, t_scaled, obuf, acc, ar1, ar2, mine,
    loc_sem, tl_sem, ta_send, ta_recv, tb_loc, tb_send, tb_recv, tc_send, tc_recv, ts_send, ts_recv,
    c_send, c_recv, sib_send, sib_recv, a1_send, a1_recv, a2_send, a2_recv, osem,
):
    nz = n // 2
    tq = tok // ns
    c_in, t_in, outs = (c1, c2), (t1, t2), (out1, out2)
    r = lax.axis_index("replica")
    s = lax.axis_index("shard")
    z = r // 2
    core = r % 2
    sib = z * 2 + 1 - core
    layers = range(LAYERS)

    def remote(src, dst, ss, rs, dr, ds):
        return pltpu.make_async_remote_copy(
            src_ref=src, dst_ref=dst, send_sem=ss, recv_sem=rs,
            device_id=(dr, ds), device_id_type=MESH,
        )

    def rows(rep):
        return pl.ds(pl.multiple_of(rep * tok, tok), tok)

    def quarter(q):
        return pl.ds(pl.multiple_of(q * tq, tq), tq)

    def t_half(l, q, h):
        if ocols % LANES == 0:
            return t_in[l].at[quarter(q), pl.ds(h * ocols, ocols)]
        return t_in[l].at[h, quarter(q)]

    barrier = pltpu.get_barrier_semaphore()
    for q in range(ns):
        @pl.when(q != s)
        def _():
            pl.semaphore_signal(barrier, inc=1, device_id=(r, q), device_id_type=MESH)
    for rep in range(n):
        @pl.when(rep != r)
        def _():
            pl.semaphore_signal(barrier, inc=1, device_id=(rep, s), device_id_type=MESH)
    local = []
    for l in layers:
        local.append(pltpu.make_async_copy(c_in[l], c_all.at[l, rows(r)], loc_sem.at[l]))
        for h in range(2):
            local.append(pltpu.make_async_copy(t_half(l, s, h), stage.at[l, s, h], tl_sem.at[l, h]))
    for copy in local:
        copy.start()
    pl.semaphore_wait(barrier, n + ns - 2)

    def ta(l, q, h):
        return remote(t_half(l, q, h), stage.at[l, s, h], ta_send.at[l, q, h],
                      ta_recv.at[l, s, h], r, q)

    def ta_in(l, q, h):
        return remote(t_half(l, s, h), stage.at[l, q, h], ta_send.at[l, q, h],
                      ta_recv.at[l, q, h], r, q)

    def tb(l, j):
        return remote(stage.at[l, j // 2, j % 2], t_all.at[l, 0, r, quarter(s)],
                      tb_send.at[l, j], tb_recv.at[l, r], j, s)

    def tb_in(l, j):
        return remote(stage.at[l, j // 2, j % 2], t_all.at[l, 0, j, quarter(s)],
                      tb_send.at[l, j], tb_recv.at[l, j], j, s)

    def tb_own(l, j):
        return pltpu.make_async_copy(stage.at[l, j // 2, j % 2], t_all.at[l, 0, r, quarter(s)], tb_loc.at[l])

    def tc(l, q, chip):
        part = t_all.at[l, 0, pl.ds(2 * chip, 2), quarter(s)]
        return remote(part, part, tc_send.at[l, q, chip], tc_recv.at[l, s, chip], r, q)

    def tc_in(l, q, chip):
        part = t_all.at[l, 0, pl.ds(2 * chip, 2), quarter(q)]
        return remote(part, part, tc_send.at[l, q, chip], tc_recv.at[l, q, chip], r, q)

    def t_sib(l, q):
        return remote(t_all.at[l, 0, :, quarter(q)], t_all.at[l, 1, :, quarter(q)],
                      ts_send.at[l, q], ts_recv.at[l, q], sib, s)

    def c_copy(l, way, t):
        chip = z - t if way == 0 else z + t
        block = c_all.at[l, rows(2 * chip + core)]
        src = c_in[l] if t == 0 else block
        to = r + 2 if way == 0 else r - 2
        return remote(src, block, c_send.at[l, way, t], c_recv.at[l, way, t], to, s)

    def c_sends(way, t):
        if way == 0:
            return jnp.logical_and(z < nz - 1, z - t >= 0)
        return jnp.logical_and(z > 0, z + t <= nz - 1)

    def c_in_chip(way, t):
        return z - 1 - t if way == 0 else z + 1 + t

    def c_valid(way, t):
        chip = c_in_chip(way, t)
        return chip >= 0 if way == 0 else chip <= nz - 1

    def c_wait(l, way, t):
        block = c_all.at[l, rows(2 * c_in_chip(way, t) + core)]
        remote(block, block, c_send.at[l, way, t], c_recv.at[l, way, t], sib, s).wait_recv()

    def sib_out(l, chip):
        block = c_all.at[l, rows(2 * chip + core)]
        return remote(block, block, sib_send.at[l, chip], sib_recv.at[l, chip], sib, s)

    def sib_in(l, chip):
        block = c_all.at[l, rows(2 * chip + 1 - core)]
        return remote(block, block, sib_send.at[l, chip], sib_recv.at[l, chip], sib, s)

    def when_each(pairs):
        for cond, fn in pairs:
            pl.when(cond)(fn)

    def ta_start(l):
        for q in range(ns):
            for h in range(2):
                when_each([(q != s, lambda q=q, h=h: ta(l, q, h).start())])

    def own_start(l):
        for way in range(2):
            when_each([(c_sends(way, 0), lambda way=way: c_copy(l, way, 0).start())])

    def tb_start(l):
        for q in range(ns):
            for h in range(2):
                when_each([(q != s, lambda q=q, h=h: ta_in(l, q, h).wait_recv())])
        for j in range(n):
            when_each([
                (j != r, lambda j=j: tb(l, j).start()),
                (j == r, lambda j=j: tb_own(l, j).start()),
            ])

    def arrive(l, t):
        for way in range(2):
            def take(l=l, way=way, t=t):
                c_wait(l, way, t)
                if t + 1 <= nz - 2:
                    when_each([(c_sends(way, t + 1), lambda: c_copy(l, way, t + 1).start())])
                sib_out(l, c_in_chip(way, t)).start()

            when_each([(c_valid(way, t), take)])

    def share_t(l):
        for k in range(nz):
            chip = lax.rem(z + k, nz)
            if k == 0:
                tb_own(l, r).wait()
                tb_in(l, sib).wait_recv()
            else:
                tb_in(l, 2 * chip).wait_recv()
                tb_in(l, 2 * chip + 1).wait_recv()
            for q in range(ns):
                when_each([(q != s, lambda q=q, chip=chip: tc(l, q, chip).start())])
        t_sib(l, s).start()

    def gram_block(l, i, chip):
        b = 2 * chip + core
        pair = pl.ds(pl.multiple_of(i * 2 * tok, 2 * tok), 2 * tok)
        dims = (((1,), (1,)), ((), ()))
        x = lax.dot_general(c_all[l, pair, :], c_all[l, rows(b), :], dims, preferred_element_type=F32)
        y = jnp.zeros_like(x)
        for h in range(2):
            ti = t_all[l, h, pl.ds(2 * i, 2)].reshape(2 * tok, ocols)
            y = y + lax.dot_general(ti, t_all[l, h, b], dims, preferred_element_type=F32)
        p = x * y
        for da in range(2):
            a = 2 * i + da
            share = jnp.where(jnp.logical_and(i == chip, a != b), 0.5, 1.0)
            part = jnp.sum(p[da * tok : (da + 1) * tok], axis=0, keepdims=True)
            v = part[:, :LANES]
            for e in range(1, tok // LANES):
                v = v + part[:, e * LANES : (e + 1) * LANES]
            v = v * share
            acc[l, a, pl.ds(b, 1), :] = v
            acc[l, b, pl.ds(a, 1), :] = v

    def gram_step(l, t):
        lo0, hi0 = jnp.maximum(z - t, 0), jnp.minimum(z + t, nz - 1)
        lo1, hi1 = jnp.maximum(z - 1 - t, 0), jnp.minimum(z + 1 + t, nz - 1)
        down = jnp.where(lo1 < lo0, 1, 0)
        up = jnp.where(hi1 > hi0, 1, 0)
        width = hi0 - lo0 + 1
        own = 1 if t == 0 else 0

        def earlier(k, _):
            first = k < down * width
            gram_block(l, jnp.where(first, lo0 + k, lo0 + k - down * width), jnp.where(first, lo1, hi1))
            return 0

        def among(k, _):
            i = jnp.where(k < own, z, jnp.where(k < own + down, lo1, jnp.where(k < own + down + up, hi1, lo1)))
            chip = jnp.where(k < own, z, jnp.where(k < own + down, lo1, hi1))
            gram_block(l, i, chip)
            return 0

        lax.fori_loop(0, (down + up) * width, earlier, 0)
        for way in range(2):
            when_each([(c_valid(way, t), lambda way=way: sib_in(l, c_in_chip(way, t)).wait_recv())])
        lax.fori_loop(0, own + down + up + down * up, among, 0)

    def turn(l, t):
        down = jnp.where(c_valid(0, t), 1, 0)
        up = jnp.where(c_valid(1, t), 1, 0)
        own = 1 if t == 0 else 0

        def body(k, _):
            chip = jnp.where(k < own, z, jnp.where(k < own + down, z - 1 - t, z + 1 + t))
            pair = pl.ds(pl.multiple_of(chip * 2 * tok, 2 * tok), 2 * tok)
            ct_all[l, :, pair] = c_all[l, pair, :].T
            return 0

        lax.fori_loop(0, own + down + up, body, 0)

    def rows_sum_start(l):
        lane = lax.broadcasted_iota(jnp.int32, (n, LANES), 1)
        value = jnp.zeros((n, LANES), F32)
        for a in range(n):
            value = jnp.where(lane == a, jnp.sum(acc[l, a], axis=1, keepdims=True), value)
        ar1[l, s] = value
        mine[l, 0] = value
        for q in range(ns):
            when_each([(q != s, lambda q=q: remote(
                mine.at[l, 0], ar1.at[l, s], a1_send.at[l, q], a1_recv.at[l, s], r, q).start())])

    def replica_sum_start(l):
        for q in range(ns):
            when_each([(q != s, lambda q=q: remote(
                mine.at[l, 0], ar1.at[l, q], a1_send.at[l, q], a1_recv.at[l, q], r, q).wait_recv())])
        value = jnp.sum(ar1[l], axis=0)
        ar2[l, r] = value
        mine[l, 1] = value
        for j in range(n):
            when_each([(j != r, lambda j=j: remote(
                mine.at[l, 1], ar2.at[l, r], a2_send.at[l, j], a2_recv.at[l, r], j, s).start())])

    def gram_total(l):
        for j in range(n):
            when_each([(j != r, lambda j=j: remote(
                mine.at[l, 1], ar2.at[l, j], a2_send.at[l, j], a2_recv.at[l, j], j, s).wait_recv())])
        return jnp.sum(ar2[l], axis=0)

    def out_copy(l, m):
        part = pl.ds(pl.multiple_of(m * mt, mt), mt)
        return pltpu.make_async_copy(obuf.at[l, part], outs[l].at[part], osem.at[l, m])

    def finish(l):
        gram = gram_total(l) * (1.0 / (float(tok) * float(tok)))
        weights = replica_weights(gram, n) * (1.0 / float(tok))
        for rep in range(n):
            w = jnp.broadcast_to(weights[rep : rep + 1, :], (tok, ocols))
            t_scaled[rep * tok : (rep + 1) * tok, :] = (t_all[l, 0, rep].astype(F32) * w).astype(jnp.bfloat16)

        def body(m, _):
            part = pl.ds(pl.multiple_of(m * mt, mt), mt)
            obuf[l, part, :] = lax.dot_general(
                ct_all[l, part, :], t_scaled[...], (((1,), (0,)), ((), ())),
                preferred_element_type=F32,
            ).astype(jnp.bfloat16)
            out_copy(l, m).start()
            return 0

        lax.fori_loop(0, cols // mt, body, 0)

    def inputs_ready(l):
        for q in range(ns):
            def pass_on(q=q):
                for chip in range(nz):
                    tc_in(l, q, chip).wait_recv()
                t_sib(l, q).start()

            when_each([(q != s, pass_on)])
        sib_in(l, z).wait_recv()
        for q in range(ns):
            t_sib(l, q).wait_recv()

    last = nz - 2
    at_end = jnp.logical_or(z == 0, z == nz - 1)
    ta_start(0)
    own_start(0)
    acc[...] = jnp.zeros_like(acc)
    for copy in local:
        copy.wait()
    for l in layers:
        sib_out(l, z).start()
    tb_start(0)
    ta_start(1)
    arrive(0, 0)
    share_t(0)
    tb_start(1)
    for t in range(1, last):
        arrive(0, t)
    own_start(1)
    share_t(1)
    for t in range(last - 1):
        arrive(1, t)
    when_each([(jnp.logical_not(at_end), lambda: arrive(1, last - 1))])
    inputs_ready(0)
    for t in range(last):
        gram_step(0, t)
        turn(0, t)
    arrive(0, last)
    gram_step(0, last)
    rows_sum_start(0)
    turn(0, last)
    inputs_ready(1)
    gram_step(1, 0)
    replica_sum_start(0)
    turn(1, 0)
    finish(0)
    when_each([(at_end, lambda: arrive(1, last - 1))])
    for t in range(1, last):
        gram_step(1, t)
        turn(1, t)
    arrive(1, last)
    gram_step(1, last)
    rows_sum_start(1)
    turn(1, last)
    replica_sum_start(1)
    finish(1)

    for l in layers:
        for q in range(ns):
            def drain(l=l, q=q):
                for h in range(2):
                    ta(l, q, h).wait_send()
                for chip in range(nz):
                    tc(l, q, chip).wait_send()
                remote(mine.at[l, 0], ar1.at[l, s], a1_send.at[l, q], a1_recv.at[l, s], r, q).wait_send()

            when_each([(q != s, drain)])
        for j in range(n):
            def drain_b(l=l, j=j):
                tb(l, j).wait_send()
                remote(mine.at[l, 1], ar2.at[l, r], a2_send.at[l, j], a2_recv.at[l, r], j, s).wait_send()

            when_each([(j != r, drain_b)])
        sib_out(l, z).wait_send()
        for q in range(ns):
            t_sib(l, q).wait_send()
        for t in range(nz - 1):
            for way in range(2):
                when_each([
                    (c_sends(way, t), lambda l=l, way=way, t=t: c_copy(l, way, t).wait_send()),
                    (c_valid(way, t), lambda l=l, way=way, t=t: sib_out(l, c_in_chip(way, t)).wait_send()),
                ])
        for m in range(cols // mt):
            out_copy(l, m).wait()


def solution(mesh):
    n, ns = mesh.shape["replica"], mesh.shape["shard"]

    def shards(context_one, cotangent_one, context_two, cotangent_two):
        tok, cols = context_one.shape
        ocols = cols * ns // n
        mt = 256 if cols % 256 == 0 else cols
        nz = n // 2

        def halves(t):
            if ocols % LANES == 0:
                return t
            return t.reshape(tok, 2, ocols).transpose(1, 0, 2)

        dma = lambda *shape: pltpu.SemaphoreType.DMA(shape)
        bf = jnp.bfloat16
        any_spec = pl.BlockSpec(memory_space=pl.ANY)
        flops = LAYERS * 2 * n * tok * (cols * ocols + n * tok * (cols + ocols) // 2)
        combined = pl.pallas_call(
            functools.partial(kernel, n, ns, tok, cols, ocols, mt),
            out_shape=[jax.ShapeDtypeStruct((cols, ocols), bf)] * 2,
            in_specs=[any_spec] * 4,
            out_specs=[any_spec] * 2,
            scratch_shapes=[
                pltpu.VMEM((LAYERS, n * tok, cols), bf),
                pltpu.VMEM((LAYERS, cols, n * tok), bf),
                pltpu.VMEM((LAYERS, 2, n, tok, ocols), bf),
                pltpu.VMEM((LAYERS, ns, 2, tok // ns, ocols), bf),
                pltpu.VMEM((n * tok, ocols), bf),
                pltpu.VMEM((LAYERS, cols, ocols), bf),
                pltpu.VMEM((LAYERS, n, n, LANES), F32),
                pltpu.VMEM((LAYERS, ns, n, LANES), F32),
                pltpu.VMEM((LAYERS, n, n, LANES), F32),
                pltpu.VMEM((LAYERS, 2, n, LANES), F32),
                dma(LAYERS), dma(LAYERS, 2),
                dma(LAYERS, ns, 2), dma(LAYERS, ns, 2),
                dma(LAYERS), dma(LAYERS, n), dma(LAYERS, n),
                dma(LAYERS, ns, nz), dma(LAYERS, ns, nz), dma(LAYERS, ns), dma(LAYERS, ns),
                dma(LAYERS, 2, nz), dma(LAYERS, 2, nz),
                dma(LAYERS, nz), dma(LAYERS, nz),
                dma(LAYERS, ns), dma(LAYERS, ns),
                dma(LAYERS, n), dma(LAYERS, n),
                dma(LAYERS, cols // mt),
            ],
            compiler_params=pltpu.CompilerParams(
                collective_id=0, has_side_effects=True, vmem_limit_bytes=56 * 2**20
            ),
            cost_estimate=pl.CostEstimate(
                flops=flops, transcendentals=0,
                bytes_accessed=LAYERS * (2 * tok * cols * 2 + cols * ocols * 2),
            ),
        )(context_one, halves(cotangent_one), context_two, halves(cotangent_two))
        return tuple(value.astype(F32) for value in combined)

    return jax.shard_map(
        shards,
        mesh=mesh,
        in_specs=(P("replica", "shard"),) * 4,
        out_specs=(P("shard", "replica"),) * 2,
        check_vma=False,
    )
```

```python
import functools

import jax
import jax.numpy as jnp
from jax import lax
from jax.experimental import pallas as pl
from jax.experimental.pallas import tpu as pltpu
from jax.sharding import PartitionSpec as P

EPSILON = 1e-06
MESH = pl.DeviceIdType.MESH
LAYERS = 2
LANES = 128
F32 = jnp.float32


def pair_coefficient(inner, own_sq, other_sq):
    own_sq = jnp.maximum(own_sq, 0.0)
    bound = jnp.sqrt(own_sq) * jnp.sqrt(jnp.maximum(other_sq, 0.0))
    inner = jnp.clip(inner, -bound, bound)
    return 1.0 - inner / (2.0 * (own_sq + EPSILON))


def replica_weights(gram, n):
    row = lax.broadcasted_iota(jnp.int32, gram.shape, 0)
    lane = lax.broadcasted_iota(jnp.int32, gram.shape, 1)
    col_w = jnp.ones((n, 1), F32)
    row_w = jnp.ones((1, LANES), F32)
    for level in range(n.bit_length() - 1):
        same = (row >> level) == (lane >> level)
        other = (row >> level) == ((lane >> level) ^ 1)
        scaled = gram * col_w * row_w
        inside = jnp.where(same, scaled, 0.0)
        across = jnp.where(other, scaled, 0.0)
        in_row = jnp.sum(inside, axis=0, keepdims=True)
        ac_row = jnp.sum(across, axis=0, keepdims=True)
        in_col = jnp.sum(inside, axis=1, keepdims=True)
        ac_col = jnp.sum(across, axis=1, keepdims=True)

        def total(mask, value, axis):
            return jnp.sum(jnp.where(mask, value, 0.0), axis=axis, keepdims=True)

        col_w = col_w * pair_coefficient(
            total(same, ac_row, 1), total(same, in_row, 1), total(other, in_row, 1)
        )
        row_w = row_w * pair_coefficient(
            total(same, ac_col, 0), total(same, in_col, 0), total(other, in_col, 0)
        )
    return col_w


def kernel(
    n, ns, tok, cols, ocols, mt,
    c1, t1, c2, t2, out1, out2,
    c_all, ct_all, t_all, stage, t_scaled, obuf, acc, ar1, ar2, mine,
    loc_sem, tl_sem, ta_send, ta_recv, tb_loc, tb_send, tb_recv, tc_send, tc_recv, ts_send, ts_recv,
    c_send, c_recv, sib_send, sib_recv, a1_send, a1_recv, a2_send, a2_recv, osem,
):
    nz = n // 2
    tq = tok // ns
    c_in, t_in, outs = (c1, c2), (t1, t2), (out1, out2)
    r = lax.axis_index("replica")
    s = lax.axis_index("shard")
    z = r // 2
    core = r % 2
    sib = z * 2 + 1 - core
    layers = range(LAYERS)

    def remote(src, dst, ss, rs, dr, ds):
        return pltpu.make_async_remote_copy(
            src_ref=src, dst_ref=dst, send_sem=ss, recv_sem=rs,
            device_id=(dr, ds), device_id_type=MESH,
        )

    def rows(rep):
        return pl.ds(pl.multiple_of(rep * tok, tok), tok)

    def quarter(q):
        return pl.ds(pl.multiple_of(q * tq, tq), tq)

    def t_half(l, q, h):
        if ocols % LANES == 0:
            return t_in[l].at[quarter(q), pl.ds(h * ocols, ocols)]
        return t_in[l].at[h, quarter(q)]

    barrier = pltpu.get_barrier_semaphore()
    for q in range(ns):
        @pl.when(q != s)
        def _():
            pl.semaphore_signal(barrier, inc=1, device_id=(r, q), device_id_type=MESH)
    for rep in range(n):
        @pl.when(rep != r)
        def _():
            pl.semaphore_signal(barrier, inc=1, device_id=(rep, s), device_id_type=MESH)
    local = []
    for l in layers:
        local.append(pltpu.make_async_copy(c_in[l], c_all.at[l, rows(r)], loc_sem.at[l]))
        for h in range(2):
            local.append(pltpu.make_async_copy(t_half(l, s, h), stage.at[l, s, h], tl_sem.at[l, h]))
    for copy in local:
        copy.start()
    pl.semaphore_wait(barrier, n + ns - 2)

    def ta(l, q, h):
        return remote(t_half(l, q, h), stage.at[l, s, h], ta_send.at[l, q, h],
                      ta_recv.at[l, s, h], r, q)

    def ta_in(l, q, h):
        return remote(t_half(l, s, h), stage.at[l, q, h], ta_send.at[l, q, h],
                      ta_recv.at[l, q, h], r, q)

    def tb(l, j):
        return remote(stage.at[l, j // 2, j % 2], t_all.at[l, 0, r, quarter(s)],
                      tb_send.at[l, j], tb_recv.at[l, r], j, s)

    def tb_in(l, j):
        return remote(stage.at[l, j // 2, j % 2], t_all.at[l, 0, j, quarter(s)],
                      tb_send.at[l, j], tb_recv.at[l, j], j, s)

    def tb_own(l, j):
        return pltpu.make_async_copy(stage.at[l, j // 2, j % 2], t_all.at[l, 0, r, quarter(s)], tb_loc.at[l])

    def tc(l, q, chip):
        part = t_all.at[l, 0, pl.ds(2 * chip, 2), quarter(s)]
        return remote(part, part, tc_send.at[l, q, chip], tc_recv.at[l, s, chip], r, q)

    def tc_in(l, q, chip):
        part = t_all.at[l, 0, pl.ds(2 * chip, 2), quarter(q)]
        return remote(part, part, tc_send.at[l, q, chip], tc_recv.at[l, q, chip], r, q)

    def t_sib(l, q):
        return remote(t_all.at[l, 0, :, quarter(q)], t_all.at[l, 1, :, quarter(q)],
                      ts_send.at[l, q], ts_recv.at[l, q], sib, s)

    def half_rows(rep, half):
        start = pl.multiple_of(rep * tok + half * (tok // 2), tok // 2)
        return pl.ds(start, tok // 2)

    def c_copy(l, way, t, half):
        chip = z - t if way == 0 else z + t
        block = c_all.at[l, half_rows(2 * chip + core, half)]
        src = c_in[l].at[pl.ds(half * (tok // 2), tok // 2)] if t == 0 else block
        to = r + 2 if way == 0 else r - 2
        return remote(src, block, c_send.at[l, way, t, half], c_recv.at[l, way, t, half], to, s)

    def c_sends(way, t):
        if way == 0:
            return jnp.logical_and(z < nz - 1, z - t >= 0)
        return jnp.logical_and(z > 0, z + t <= nz - 1)

    def c_in_chip(way, t):
        return z - 1 - t if way == 0 else z + 1 + t

    def c_valid(way, t):
        chip = c_in_chip(way, t)
        return chip >= 0 if way == 0 else chip <= nz - 1

    def c_wait(l, way, t, half):
        block = c_all.at[l, half_rows(2 * c_in_chip(way, t) + core, half)]
        remote(block, block, c_send.at[l, way, t, half], c_recv.at[l, way, t, half], sib, s).wait_recv()

    def sib_out(l, chip):
        block = c_all.at[l, rows(2 * chip + core)]
        return remote(block, block, sib_send.at[l, chip], sib_recv.at[l, chip], sib, s)

    def sib_in(l, chip):
        block = c_all.at[l, rows(2 * chip + 1 - core)]
        return remote(block, block, sib_send.at[l, chip], sib_recv.at[l, chip], sib, s)

    def when_each(pairs):
        for cond, fn in pairs:
            pl.when(cond)(fn)

    def ta_start(l):
        for q in range(ns):
            for h in range(2):
                when_each([(q != s, lambda q=q, h=h: ta(l, q, h).start())])

    def own_start(l):
        for way in range(2):
            for half in range(2):
                when_each([(c_sends(way, 0), lambda way=way, half=half: c_copy(l, way, 0, half).start())])

    def tb_start(l):
        for q in range(ns):
            for h in range(2):
                when_each([(q != s, lambda q=q, h=h: ta_in(l, q, h).wait_recv())])
        for j in range(n):
            when_each([
                (j != r, lambda j=j: tb(l, j).start()),
                (j == r, lambda j=j: tb_own(l, j).start()),
            ])

    def arrive(l, t):
        for half in range(2):
            for way in range(2):
                def take(way=way, half=half):
                    c_wait(l, way, t, half)
                    if t + 1 <= nz - 2:
                        when_each([(c_sends(way, t + 1), lambda: c_copy(l, way, t + 1, half).start())])
                    if half == 1:
                        sib_out(l, c_in_chip(way, t)).start()

                when_each([(c_valid(way, t), take)])

    def share_t(l):
        for k in range(nz):
            chip = lax.rem(z + k, nz)
            if k == 0:
                tb_own(l, r).wait()
                tb_in(l, sib).wait_recv()
            else:
                tb_in(l, 2 * chip).wait_recv()
                tb_in(l, 2 * chip + 1).wait_recv()
            for q in range(ns):
                when_each([(q != s, lambda q=q, chip=chip: tc(l, q, chip).start())])
        t_sib(l, s).start()

    def gram_block(l, i, chip):
        b = 2 * chip + core
        pair = pl.ds(pl.multiple_of(i * 2 * tok, 2 * tok), 2 * tok)
        dims = (((1,), (1,)), ((), ()))
        x = lax.dot_general(c_all[l, pair, :], c_all[l, rows(b), :], dims, preferred_element_type=F32)
        y = jnp.zeros_like(x)
        for h in range(2):
            ti = t_all[l, h, pl.ds(2 * i, 2)].reshape(2 * tok, ocols)
            y = y + lax.dot_general(ti, t_all[l, h, b], dims, preferred_element_type=F32)
        p = x * y
        for da in range(2):
            a = 2 * i + da
            share = jnp.where(jnp.logical_and(i == chip, a != b), 0.5, 1.0)
            part = jnp.sum(p[da * tok : (da + 1) * tok], axis=0, keepdims=True)
            v = part[:, :LANES]
            for e in range(1, tok // LANES):
                v = v + part[:, e * LANES : (e + 1) * LANES]
            v = v * share
            acc[l, a, pl.ds(b, 1), :] = v
            acc[l, b, pl.ds(a, 1), :] = v

    def gram_step(l, t):
        lo0, hi0 = jnp.maximum(z - t, 0), jnp.minimum(z + t, nz - 1)
        lo1, hi1 = jnp.maximum(z - 1 - t, 0), jnp.minimum(z + 1 + t, nz - 1)
        down = jnp.where(lo1 < lo0, 1, 0)
        up = jnp.where(hi1 > hi0, 1, 0)
        width = hi0 - lo0 + 1
        own = 1 if t == 0 else 0

        def earlier(k, _):
            first = k < down * width
            gram_block(l, jnp.where(first, lo0 + k, lo0 + k - down * width), jnp.where(first, lo1, hi1))
            return 0

        def among(k, _):
            i = jnp.where(k < own, z, jnp.where(k < own + down, lo1, jnp.where(k < own + down + up, hi1, lo1)))
            chip = jnp.where(k < own, z, jnp.where(k < own + down, lo1, hi1))
            gram_block(l, i, chip)
            return 0

        lax.fori_loop(0, (down + up) * width, earlier, 0)
        for way in range(2):
            when_each([(c_valid(way, t), lambda way=way: sib_in(l, c_in_chip(way, t)).wait_recv())])
        lax.fori_loop(0, own + down + up + down * up, among, 0)

    def turn(l, t):
        down = jnp.where(c_valid(0, t), 1, 0)
        up = jnp.where(c_valid(1, t), 1, 0)
        own = 1 if t == 0 else 0

        def body(k, _):
            chip = jnp.where(k < own, z, jnp.where(k < own + down, z - 1 - t, z + 1 + t))
            pair = pl.ds(pl.multiple_of(chip * 2 * tok, 2 * tok), 2 * tok)
            ct_all[l, :, pair] = c_all[l, pair, :].T
            return 0

        lax.fori_loop(0, own + down + up, body, 0)

    def rows_sum_start(l):
        lane = lax.broadcasted_iota(jnp.int32, (n, LANES), 1)
        value = jnp.zeros((n, LANES), F32)
        for a in range(n):
            value = jnp.where(lane == a, jnp.sum(acc[l, a], axis=1, keepdims=True), value)
        ar1[l, s] = value
        mine[l, 0] = value
        for q in range(ns):
            when_each([(q != s, lambda q=q: remote(
                mine.at[l, 0], ar1.at[l, s], a1_send.at[l, q], a1_recv.at[l, s], r, q).start())])

    def replica_sum_start(l):
        for q in range(ns):
            when_each([(q != s, lambda q=q: remote(
                mine.at[l, 0], ar1.at[l, q], a1_send.at[l, q], a1_recv.at[l, q], r, q).wait_recv())])
        value = jnp.sum(ar1[l], axis=0)
        ar2[l, r] = value
        mine[l, 1] = value
        for j in range(n):
            when_each([(j != r, lambda j=j: remote(
                mine.at[l, 1], ar2.at[l, r], a2_send.at[l, j], a2_recv.at[l, r], j, s).start())])

    def gram_total(l):
        for j in range(n):
            when_each([(j != r, lambda j=j: remote(
                mine.at[l, 1], ar2.at[l, j], a2_send.at[l, j], a2_recv.at[l, j], j, s).wait_recv())])
        return jnp.sum(ar2[l], axis=0)

    def out_copy(l, m):
        part = pl.ds(pl.multiple_of(m * mt, mt), mt)
        return pltpu.make_async_copy(obuf.at[l, part], outs[l].at[part], osem.at[l, m])

    def finish(l):
        gram = gram_total(l) * (1.0 / (float(tok) * float(tok)))
        weights = replica_weights(gram, n) * (1.0 / float(tok))
        for rep in range(n):
            w = jnp.broadcast_to(weights[rep : rep + 1, :], (tok, ocols))
            t_scaled[rep * tok : (rep + 1) * tok, :] = (t_all[l, 0, rep].astype(F32) * w).astype(jnp.bfloat16)

        def body(m, _):
            part = pl.ds(pl.multiple_of(m * mt, mt), mt)
            obuf[l, part, :] = lax.dot_general(
                ct_all[l, part, :], t_scaled[...], (((1,), (0,)), ((), ())),
                preferred_element_type=F32,
            ).astype(jnp.bfloat16)
            out_copy(l, m).start()
            return 0

        lax.fori_loop(0, cols // mt, body, 0)

    def inputs_ready(l):
        for q in range(ns):
            def pass_on(q=q):
                for chip in range(nz):
                    tc_in(l, q, chip).wait_recv()
                t_sib(l, q).start()

            when_each([(q != s, pass_on)])
        sib_in(l, z).wait_recv()
        for q in range(ns):
            t_sib(l, q).wait_recv()

    last = nz - 2
    at_end = jnp.logical_or(z == 0, z == nz - 1)
    ta_start(0)
    own_start(0)
    acc[...] = jnp.zeros_like(acc)
    for copy in local:
        copy.wait()
    for l in layers:
        sib_out(l, z).start()
    tb_start(0)
    ta_start(1)
    own_start(1)
    arrive(0, 0)
    tb_start(1)
    arrive(1, 0)
    share_t(0)
    for t in range(1, last):
        arrive(0, t)
        if t == 1:
            share_t(1)
        if t < last - 1:
            arrive(1, t)
    when_each([(jnp.logical_not(at_end), lambda: arrive(1, last - 1))])
    inputs_ready(0)
    for t in range(last):
        gram_step(0, t)
        turn(0, t)
    when_each([(at_end, lambda: arrive(1, last - 1))])
    inputs_ready(1)
    for t in range(last):
        gram_step(1, t)
        turn(1, t)
    arrive(0, last)
    gram_step(0, last)
    rows_sum_start(0)
    turn(0, last)
    replica_sum_start(0)
    arrive(1, last)
    gram_step(1, last)
    rows_sum_start(1)
    turn(1, last)
    finish(0)
    replica_sum_start(1)
    finish(1)

    for l in layers:
        for q in range(ns):
            def drain(l=l, q=q):
                for h in range(2):
                    ta(l, q, h).wait_send()
                for chip in range(nz):
                    tc(l, q, chip).wait_send()
                remote(mine.at[l, 0], ar1.at[l, s], a1_send.at[l, q], a1_recv.at[l, s], r, q).wait_send()

            when_each([(q != s, drain)])
        for j in range(n):
            def drain_b(l=l, j=j):
                tb(l, j).wait_send()
                remote(mine.at[l, 1], ar2.at[l, r], a2_send.at[l, j], a2_recv.at[l, r], j, s).wait_send()

            when_each([(j != r, drain_b)])
        sib_out(l, z).wait_send()
        for q in range(ns):
            t_sib(l, q).wait_send()
        for t in range(nz - 1):
            for way in range(2):
                for half in range(2):
                    when_each([(c_sends(way, t), lambda l=l, way=way, t=t, half=half: c_copy(l, way, t, half).wait_send())])
                when_each([
                    (c_valid(way, t), lambda l=l, way=way, t=t: sib_out(l, c_in_chip(way, t)).wait_send()),
                ])
        for m in range(cols // mt):
            out_copy(l, m).wait()


def solution(mesh):
    n, ns = mesh.shape["replica"], mesh.shape["shard"]

    def shards(context_one, cotangent_one, context_two, cotangent_two):
        tok, cols = context_one.shape
        ocols = cols * ns // n
        mt = 256 if cols % 256 == 0 else cols
        nz = n // 2

        def halves(t):
            if ocols % LANES == 0:
                return t
            return t.reshape(tok, 2, ocols).transpose(1, 0, 2)

        dma = lambda *shape: pltpu.SemaphoreType.DMA(shape)
        bf = jnp.bfloat16
        any_spec = pl.BlockSpec(memory_space=pl.ANY)
        flops = LAYERS * 2 * n * tok * (cols * ocols + n * tok * (cols + ocols) // 2)
        combined = pl.pallas_call(
            functools.partial(kernel, n, ns, tok, cols, ocols, mt),
            out_shape=[jax.ShapeDtypeStruct((cols, ocols), bf)] * 2,
            in_specs=[any_spec] * 4,
            out_specs=[any_spec] * 2,
            scratch_shapes=[
                pltpu.VMEM((LAYERS, n * tok, cols), bf),
                pltpu.VMEM((LAYERS, cols, n * tok), bf),
                pltpu.VMEM((LAYERS, 2, n, tok, ocols), bf),
                pltpu.VMEM((LAYERS, ns, 2, tok // ns, ocols), bf),
                pltpu.VMEM((n * tok, ocols), bf),
                pltpu.VMEM((LAYERS, cols, ocols), bf),
                pltpu.VMEM((LAYERS, n, n, LANES), F32),
                pltpu.VMEM((LAYERS, ns, n, LANES), F32),
                pltpu.VMEM((LAYERS, n, n, LANES), F32),
                pltpu.VMEM((LAYERS, 2, n, LANES), F32),
                dma(LAYERS), dma(LAYERS, 2),
                dma(LAYERS, ns, 2), dma(LAYERS, ns, 2),
                dma(LAYERS), dma(LAYERS, n), dma(LAYERS, n),
                dma(LAYERS, ns, nz), dma(LAYERS, ns, nz), dma(LAYERS, ns), dma(LAYERS, ns),
                dma(LAYERS, 2, nz, 2), dma(LAYERS, 2, nz, 2),
                dma(LAYERS, nz), dma(LAYERS, nz),
                dma(LAYERS, ns), dma(LAYERS, ns),
                dma(LAYERS, n), dma(LAYERS, n),
                dma(LAYERS, cols // mt),
            ],
            compiler_params=pltpu.CompilerParams(
                collective_id=0, has_side_effects=True, vmem_limit_bytes=56 * 2**20
            ),
            cost_estimate=pl.CostEstimate(
                flops=flops, transcendentals=0,
                bytes_accessed=LAYERS * (2 * tok * cols * 2 + cols * ocols * 2),
            ),
        )(context_one, halves(cotangent_one), context_two, halves(cotangent_two))
        return tuple(value.astype(F32) for value in combined)

    return jax.shard_map(
        shards,
        mesh=mesh,
        in_specs=(P("replica", "shard"),) * 4,
        out_specs=(P("shard", "replica"),) * 2,
        check_vma=False,
    )
```

```python
import functools

import jax
import jax.numpy as jnp
from jax import lax
from jax.experimental import pallas as pl
from jax.experimental.pallas import tpu as pltpu
from jax.sharding import PartitionSpec as P

EPSILON = 1e-06
MESH = pl.DeviceIdType.MESH
LAYERS = 2
LANES = 128
F32 = jnp.float32


def pair_coefficient(inner, own_sq, other_sq):
    own_sq = jnp.maximum(own_sq, 0.0)
    bound = jnp.sqrt(own_sq) * jnp.sqrt(jnp.maximum(other_sq, 0.0))
    inner = jnp.clip(inner, -bound, bound)
    return 1.0 - inner / (2.0 * (own_sq + EPSILON))


def replica_weights(gram, n):
    row = lax.broadcasted_iota(jnp.int32, gram.shape, 0)
    lane = lax.broadcasted_iota(jnp.int32, gram.shape, 1)
    col_w = jnp.ones((n, 1), F32)
    row_w = jnp.ones((1, LANES), F32)
    for level in range(n.bit_length() - 1):
        same = (row >> level) == (lane >> level)
        other = (row >> level) == ((lane >> level) ^ 1)
        scaled = gram * col_w * row_w
        inside = jnp.where(same, scaled, 0.0)
        across = jnp.where(other, scaled, 0.0)
        in_row = jnp.sum(inside, axis=0, keepdims=True)
        ac_row = jnp.sum(across, axis=0, keepdims=True)
        in_col = jnp.sum(inside, axis=1, keepdims=True)
        ac_col = jnp.sum(across, axis=1, keepdims=True)

        def total(mask, value, axis):
            return jnp.sum(jnp.where(mask, value, 0.0), axis=axis, keepdims=True)

        col_w = col_w * pair_coefficient(
            total(same, ac_row, 1), total(same, in_row, 1), total(other, in_row, 1)
        )
        row_w = row_w * pair_coefficient(
            total(same, ac_col, 0), total(same, in_col, 0), total(other, in_col, 0)
        )
    return col_w


def kernel(
    n, ns, tok, cols, ocols, mt,
    c1, t1, c2, t2, out1, out2,
    c_all, t_all, stage, t_scaled, obuf, acc, ar1, ar2, mine,
    loc_sem, tl_sem, ta_send, ta_recv, tb_loc, tb_send, tb_recv, tc_send, tc_recv, ts_send, ts_recv,
    c_send, c_recv, sib_send, sib_recv, a1_send, a1_recv, a2_send, a2_recv, osem,
):
    nz = n // 2
    tq = tok // ns
    c_in, t_in, outs = (c1, c2), (t1, t2), (out1, out2)
    r = lax.axis_index("replica")
    s = lax.axis_index("shard")
    z = r // 2
    core = r % 2
    sib = z * 2 + 1 - core
    layers = range(LAYERS)

    def remote(src, dst, ss, rs, dr, ds):
        return pltpu.make_async_remote_copy(
            src_ref=src, dst_ref=dst, send_sem=ss, recv_sem=rs,
            device_id=(dr, ds), device_id_type=MESH,
        )

    def rows(rep):
        return pl.ds(pl.multiple_of(rep * tok, tok), tok)

    def quarter(q):
        return pl.ds(pl.multiple_of(q * tq, tq), tq)

    def t_half(l, q, h):
        if ocols % LANES == 0:
            return t_in[l].at[quarter(q), pl.ds(h * ocols, ocols)]
        return t_in[l].at[h, quarter(q)]

    barrier = pltpu.get_barrier_semaphore()
    for q in range(ns):
        @pl.when(q != s)
        def _():
            pl.semaphore_signal(barrier, inc=1, device_id=(r, q), device_id_type=MESH)
    for rep in range(n):
        @pl.when(rep != r)
        def _():
            pl.semaphore_signal(barrier, inc=1, device_id=(rep, s), device_id_type=MESH)
    local = []
    for l in layers:
        local.append(pltpu.make_async_copy(c_in[l], c_all.at[l, rows(r)], loc_sem.at[l]))
        for h in range(2):
            local.append(pltpu.make_async_copy(t_half(l, s, h), stage.at[l, s, h], tl_sem.at[l, h]))
    for copy in local:
        copy.start()
    pl.semaphore_wait(barrier, n + ns - 2)

    def ta(l, q, h):
        return remote(t_half(l, q, h), stage.at[l, s, h], ta_send.at[l, q, h],
                      ta_recv.at[l, s, h], r, q)

    def ta_in(l, q, h):
        return remote(t_half(l, s, h), stage.at[l, q, h], ta_send.at[l, q, h],
                      ta_recv.at[l, q, h], r, q)

    def tb(l, j):
        return remote(stage.at[l, j // 2, j % 2], t_all.at[l, 0, r, quarter(s)],
                      tb_send.at[l, j], tb_recv.at[l, r], j, s)

    def tb_in(l, j):
        return remote(stage.at[l, j // 2, j % 2], t_all.at[l, 0, j, quarter(s)],
                      tb_send.at[l, j], tb_recv.at[l, j], j, s)

    def tb_own(l, j):
        return pltpu.make_async_copy(stage.at[l, j // 2, j % 2], t_all.at[l, 0, r, quarter(s)], tb_loc.at[l])

    def tc(l, q):
        part = t_all.at[l, 0, :, quarter(s)]
        return remote(part, part, tc_send.at[l, q], tc_recv.at[l, s], r, q)

    def tc_in(l, q):
        part = t_all.at[l, 0, :, quarter(q)]
        return remote(part, part, tc_send.at[l, q], tc_recv.at[l, q], r, q)

    def t_sib(l):
        return remote(t_all.at[l, 0], t_all.at[l, 1], ts_send.at[l], ts_recv.at[l], sib, s)

    def c_copy(l, way, t):
        chip = z - t if way == 0 else z + t
        block = c_all.at[l, rows(2 * chip + core)]
        src = c_in[l] if t == 0 else block
        to = r + 2 if way == 0 else r - 2
        return remote(src, block, c_send.at[l, way, t], c_recv.at[l, way, t], to, s)

    def c_sends(way, t):
        if way == 0:
            return jnp.logical_and(z < nz - 1, z - t >= 0)
        return jnp.logical_and(z > 0, z + t <= nz - 1)

    def c_in_chip(way, t):
        return z - 1 - t if way == 0 else z + 1 + t

    def c_valid(way, t):
        chip = c_in_chip(way, t)
        return chip >= 0 if way == 0 else chip <= nz - 1

    def c_wait(l, way, t):
        block = c_all.at[l, rows(2 * c_in_chip(way, t) + core)]
        remote(block, block, c_send.at[l, way, t], c_recv.at[l, way, t], sib, s).wait_recv()

    def sib_out(l, chip):
        block = c_all.at[l, rows(2 * chip + core)]
        return remote(block, block, sib_send.at[l, chip], sib_recv.at[l, chip], sib, s)

    def sib_in(l, chip):
        block = c_all.at[l, rows(2 * chip + 1 - core)]
        return remote(block, block, sib_send.at[l, chip], sib_recv.at[l, chip], sib, s)

    def when_each(pairs):
        for cond, fn in pairs:
            pl.when(cond)(fn)

    def ta_start(l):
        for q in range(ns):
            for h in range(2):
                when_each([(q != s, lambda q=q, h=h: ta(l, q, h).start())])

    def own_start(l):
        for way in range(2):
            when_each([(c_sends(way, 0), lambda way=way: c_copy(l, way, 0).start())])

    def tb_start(l):
        for q in range(ns):
            for h in range(2):
                when_each([(q != s, lambda q=q, h=h: ta_in(l, q, h).wait_recv())])
        for j in range(n):
            when_each([
                (j != r, lambda j=j: tb(l, j).start()),
                (j == r, lambda j=j: tb_own(l, j).start()),
            ])

    def arrive(l, t):
        for way in range(2):
            def take(l=l, way=way, t=t):
                c_wait(l, way, t)
                if t + 1 <= nz - 2:
                    when_each([(c_sends(way, t + 1), lambda: c_copy(l, way, t + 1).start())])
                sib_out(l, c_in_chip(way, t)).start()

            when_each([(c_valid(way, t), take)])

    def share_t(l):
        for j in range(n):
            when_each([
                (j != r, lambda l=l, j=j: tb_in(l, j).wait_recv()),
                (j == r, lambda l=l, j=j: tb_own(l, j).wait()),
            ])
        for q in range(ns):
            when_each([(q != s, lambda l=l, q=q: tc(l, q).start())])

    def gram_block(l, i, chip):
        b = 2 * chip + core
        pair = pl.ds(pl.multiple_of(i * 2 * tok, 2 * tok), 2 * tok)
        dims = (((1,), (1,)), ((), ()))
        x = lax.dot_general(c_all[l, pair, :], c_all[l, rows(b), :], dims, preferred_element_type=F32)
        y = jnp.zeros_like(x)
        for h in range(2):
            ti = t_all[l, h, pl.ds(2 * i, 2)].reshape(2 * tok, ocols)
            y = y + lax.dot_general(ti, t_all[l, h, b], dims, preferred_element_type=F32)
        p = x * y
        for da in range(2):
            a = 2 * i + da
            share = jnp.where(jnp.logical_and(i == chip, a != b), 0.5, 1.0)
            part = jnp.sum(p[da * tok : (da + 1) * tok], axis=0, keepdims=True)
            v = part[:, :LANES]
            for e in range(1, tok // LANES):
                v = v + part[:, e * LANES : (e + 1) * LANES]
            v = v * share
            acc[l, a, pl.ds(b, 1), :] = v
            acc[l, b, pl.ds(a, 1), :] = v

    def gram_step(l, t):
        lo0, hi0 = jnp.maximum(z - t, 0), jnp.minimum(z + t, nz - 1)
        lo1, hi1 = jnp.maximum(z - 1 - t, 0), jnp.minimum(z + 1 + t, nz - 1)
        down = jnp.where(lo1 < lo0, 1, 0)
        up = jnp.where(hi1 > hi0, 1, 0)
        width = hi0 - lo0 + 1
        own = 1 if t == 0 else 0

        def earlier(k, _):
            first = k < down * width
            gram_block(l, jnp.where(first, lo0 + k, lo0 + k - down * width), jnp.where(first, lo1, hi1))
            return 0

        def among(k, _):
            i = jnp.where(k < own, z, jnp.where(k < own + down, lo1, jnp.where(k < own + down + up, hi1, lo1)))
            chip = jnp.where(k < own, z, jnp.where(k < own + down, lo1, hi1))
            gram_block(l, i, chip)
            return 0

        lax.fori_loop(0, (down + up) * width, earlier, 0)
        for way in range(2):
            when_each([(c_valid(way, t), lambda way=way: sib_in(l, c_in_chip(way, t)).wait_recv())])
        lax.fori_loop(0, own + down + up + down * up, among, 0)

    def rows_sum_start(l):
        lane = lax.broadcasted_iota(jnp.int32, (n, LANES), 1)
        value = jnp.zeros((n, LANES), F32)
        for a in range(n):
            value = jnp.where(lane == a, jnp.sum(acc[l, a], axis=1, keepdims=True), value)
        ar1[l, s] = value
        mine[l, 0] = value
        for q in range(ns):
            when_each([(q != s, lambda q=q: remote(
                mine.at[l, 0], ar1.at[l, s], a1_send.at[l, q], a1_recv.at[l, s], r, q).start())])

    def replica_sum_start(l):
        for q in range(ns):
            when_each([(q != s, lambda q=q: remote(
                mine.at[l, 0], ar1.at[l, q], a1_send.at[l, q], a1_recv.at[l, q], r, q).wait_recv())])
        value = jnp.sum(ar1[l], axis=0)
        ar2[l, r] = value
        mine[l, 1] = value
        for j in range(n):
            when_each([(j != r, lambda j=j: remote(
                mine.at[l, 1], ar2.at[l, r], a2_send.at[l, j], a2_recv.at[l, r], j, s).start())])

    def gram_total(l):
        for j in range(n):
            when_each([(j != r, lambda j=j: remote(
                mine.at[l, 1], ar2.at[l, j], a2_send.at[l, j], a2_recv.at[l, j], j, s).wait_recv())])
        return jnp.sum(ar2[l], axis=0)

    def out_copy(l, m):
        part = pl.ds(pl.multiple_of(m * mt, mt), mt)
        return pltpu.make_async_copy(obuf.at[l, part], outs[l].at[part], osem.at[l, m])

    def finish(l):
        gram = gram_total(l) * (1.0 / (float(tok) * float(tok)))
        weights = replica_weights(gram, n) * (1.0 / float(tok))
        for rep in range(n):
            w = jnp.broadcast_to(weights[rep : rep + 1, :], (tok, ocols))
            t_scaled[rep * tok : (rep + 1) * tok, :] = (t_all[l, 0, rep].astype(F32) * w).astype(jnp.bfloat16)

        def body(m, _):
            part = pl.ds(pl.multiple_of(m * mt, mt), mt)
            obuf[l, part, :] = lax.dot_general(
                c_all[l, :, part] if mt != cols else c_all[l],
                t_scaled[...], (((0,), (0,)), ((), ())), preferred_element_type=F32,
            ).astype(jnp.bfloat16)
            out_copy(l, m).start()
            return 0

        lax.fori_loop(0, cols // mt, body, 0)

    def inputs_ready(l):
        for q in range(ns):
            when_each([(q != s, lambda q=q: tc_in(l, q).wait_recv())])
        t_sib(l).start()
        sib_in(l, z).wait_recv()
        t_sib(l).wait_recv()

    last = nz - 2
    at_end = jnp.logical_or(z == 0, z == nz - 1)
    ta_start(0)
    own_start(0)
    ta_start(1)
    own_start(1)
    acc[...] = jnp.zeros_like(acc)
    for copy in local:
        copy.wait()
    for l in layers:
        sib_out(l, z).start()
    tb_start(0)
    tb_start(1)
    arrive(0, 0)
    share_t(0)
    if last > 1:
        arrive(1, 0)
    share_t(1)
    for t in range(1, last):
        arrive(0, t)
        if t < last - 1:
            arrive(1, t)
    when_each([(jnp.logical_not(at_end), lambda: arrive(1, last - 1))])
    inputs_ready(0)
    for t in range(last):
        gram_step(0, t)
    arrive(0, last)
    gram_step(0, last)
    rows_sum_start(0)
    inputs_ready(1)
    gram_step(1, 0)
    replica_sum_start(0)
    when_each([(at_end, lambda: arrive(1, last - 1))])
    for t in range(1, last):
        gram_step(1, t)
    finish(0)
    arrive(1, last)
    gram_step(1, last)
    rows_sum_start(1)
    replica_sum_start(1)
    finish(1)

    for l in layers:
        for q in range(ns):
            def drain(l=l, q=q):
                for h in range(2):
                    ta(l, q, h).wait_send()
                tc(l, q).wait_send()
                remote(mine.at[l, 0], ar1.at[l, s], a1_send.at[l, q], a1_recv.at[l, s], r, q).wait_send()

            when_each([(q != s, drain)])
        for j in range(n):
            def drain_b(l=l, j=j):
                tb(l, j).wait_send()
                remote(mine.at[l, 1], ar2.at[l, r], a2_send.at[l, j], a2_recv.at[l, r], j, s).wait_send()

            when_each([(j != r, drain_b)])
        sib_out(l, z).wait_send()
        t_sib(l).wait_send()
        for t in range(nz - 1):
            for way in range(2):
                when_each([
                    (c_sends(way, t), lambda l=l, way=way, t=t: c_copy(l, way, t).wait_send()),
                    (c_valid(way, t), lambda l=l, way=way, t=t: sib_out(l, c_in_chip(way, t)).wait_send()),
                ])
        for m in range(cols // mt):
            out_copy(l, m).wait()


def solution(mesh):
    n, ns = mesh.shape["replica"], mesh.shape["shard"]

    def shards(context_one, cotangent_one, context_two, cotangent_two):
        tok, cols = context_one.shape
        ocols = cols * ns // n
        mt = 256 if cols % 256 == 0 else cols
        nz = n // 2

        def halves(t):
            if ocols % LANES == 0:
                return t
            return t.reshape(tok, 2, ocols).transpose(1, 0, 2)

        dma = lambda *shape: pltpu.SemaphoreType.DMA(shape)
        bf = jnp.bfloat16
        any_spec = pl.BlockSpec(memory_space=pl.ANY)
        flops = LAYERS * 2 * n * tok * (cols * ocols + n * tok * (cols + ocols) // 2)
        combined = pl.pallas_call(
            functools.partial(kernel, n, ns, tok, cols, ocols, mt),
            out_shape=[jax.ShapeDtypeStruct((cols, ocols), bf)] * 2,
            in_specs=[any_spec] * 4,
            out_specs=[any_spec] * 2,
            scratch_shapes=[
                pltpu.VMEM((LAYERS, n * tok, cols), bf),
                pltpu.VMEM((LAYERS, 2, n, tok, ocols), bf),
                pltpu.VMEM((LAYERS, ns, 2, tok // ns, ocols), bf),
                pltpu.VMEM((n * tok, ocols), bf),
                pltpu.VMEM((LAYERS, cols, ocols), bf),
                pltpu.VMEM((LAYERS, n, n, LANES), F32),
                pltpu.VMEM((LAYERS, ns, n, LANES), F32),
                pltpu.VMEM((LAYERS, n, n, LANES), F32),
                pltpu.VMEM((LAYERS, 2, n, LANES), F32),
                dma(LAYERS), dma(LAYERS, 2),
                dma(LAYERS, ns, 2), dma(LAYERS, ns, 2),
                dma(LAYERS), dma(LAYERS, n), dma(LAYERS, n),
                dma(LAYERS, ns), dma(LAYERS, ns), dma(LAYERS), dma(LAYERS),
                dma(LAYERS, 2, nz), dma(LAYERS, 2, nz),
                dma(LAYERS, nz), dma(LAYERS, nz),
                dma(LAYERS, ns), dma(LAYERS, ns),
                dma(LAYERS, n), dma(LAYERS, n),
                dma(LAYERS, cols // mt),
            ],
            compiler_params=pltpu.CompilerParams(
                collective_id=0, has_side_effects=True, vmem_limit_bytes=56 * 2**20
            ),
            cost_estimate=pl.CostEstimate(
                flops=flops, transcendentals=0,
                bytes_accessed=LAYERS * (2 * tok * cols * 2 + cols * ocols * 2),
            ),
        )(context_one, halves(cotangent_one), context_two, halves(cotangent_two))
        return tuple(value.astype(F32) for value in combined)

    return jax.shard_map(
        shards,
        mesh=mesh,
        in_specs=(P("replica", "shard"),) * 4,
        out_specs=(P("shard", "replica"),) * 2,
        check_vma=False,
    )
```
